256 devices in a mesh: group: 2 (over core), seq: 16 (over y, x), head: 8 (over z).
Axes of the slice: x: 4, y: 4, z: 8, core: 2. Of those that a mesh axis runs over, the one named last changes fastest.
Arguments:
- x_in: bfloat16 [24576, 8192], P(('group', 'seq'), 'head'), parts along dimension 0, may hold values from -6 to 6
- bc_in: bfloat16 [24576, 8, 512], P(('group', 'seq'), 'head'), parts along dimension 0, may hold values from -6 to 6
- dt_in: float32 [24576, 128], P(('group', 'seq'), 'head'), parts along dimension 0, may hold values from -5 to 5
- conv_x: float32 [4, 8192], P(None, 'head'), may hold values from -3 to 3
- conv_bc: float32 [4, 8, 512], P(None, 'head'), may hold values from -3 to 3
- a_log: float32 [128], P('head'), may hold values from -11 to -2.5
- dt_bias: float32 [128], P('head'), may hold values from -1 to 1
- d_skip: float32 [128], P('head'), may hold values from 0.5 to 1.5
- norm_gain: float32 [8192], P('head'), may hold values from 0.5 to 1.5
- doc_lengths: int32 [16], P('group'), parts along dimension 0, may hold values from 1 to 9216, 12288 in all
- dec_x: bfloat16 [32, 8, 8192], P(('group', 'seq'), None, 'head'), parts along dimension 0, may hold values from -6 to 6
- dec_bc: bfloat16 [32, 8, 8, 512], P(('group', 'seq'), None, 'head'), parts along dimension 0, may hold values from -6 to 6
- dec_dt: float32 [32, 8, 128], P(('group', 'seq'), None, 'head'), parts along dimension 0, may hold values from -5 to 5
Outputs:
- prompt_out: bfloat16 [24576, 8192], P(('group', 'seq'), 'head'), parts along dimension 0
- decode_out: bfloat16 [32, 8, 8192], P(('group', 'seq'), None, 'head'), parts along dimension 0
The draws below stay inside these ranges and needn't reach their ends.
There are 2 independent parts, one for each index of `group`. The reference program is written for one: setup_inputs(seed, part) draws one part's arguments, and reference() takes and returns one part's arrays. A program takes and returns all parts, laid end to end along the dimension named above; an argument that names none is the same for every part. Nothing has to cross between parts.
Inputs may be any that keep to these rules, and one draw needn't show every extreme that they name: `doc_lengths`: the samples continue the last of the 8 documents.
All inputs are finite; a program needn't handle non-finite values.
Results may differ from the reference program's by a relative error of at most 0.0035.
Values may be sent and summed in bfloat16 or wider, within the bound.
A program may use at most 128 MiB of HBM per device.

```python
import math
import jax
import jax.numpy as jnp
import numpy as np
from jax import lax

HEADS = 128
HEAD_DIM = 64
STATE = 256
GROUPS = 8
CONV = 4
BLOCK = 256
DOCS = 8
STEPS = 8
TOKENS = 12288
INNER = 8192
CONTINUATIONS_N = 16


def draw_a_log(key, part):
    key = jax.random.fold_in(key, 7)
    key_pick, key_slow, key_fast = jax.random.split(key, 3)
    slow_share = 0.5
    fast_low = math.log(2.0 / TOKENS)
    fast_high = math.log(1.0 / 25.0)
    picked = jax.random.uniform(key_pick, (HEADS,), jnp.float32) < slow_share
    slow_value = jax.random.uniform(key_slow, (HEADS,), jnp.float32, math.log(0.3 / TOKENS), math.log(2.0 / TOKENS))
    fast_value = jax.random.uniform(key_fast, (HEADS,), jnp.float32, fast_low, fast_high)
    return jnp.where(picked, slow_value, fast_value).astype(jnp.float32)


def draw_dt_in(key, part):
    key = jax.random.fold_in(key, 11)
    values = jax.random.truncated_normal(key, -5.0, 5.0, (TOKENS, HEADS), jnp.float32)
    return values.astype(jnp.float32)


def steps_of(own_key, dims, shards, low, high):
    gain, own = 1.0, jax.random.fold_in(own_key, 6)
    for axis_at, shards_of in shards:
        draws = jnp.exp(jax.random.uniform(jax.random.fold_in(own, axis_at), (shards_of,), jnp.float32, low / len(shards), high / len(shards)))
        gain = gain * jnp.repeat(draws, dims[axis_at] // shards_of).reshape([-1 if axis == axis_at else 1 for axis in range(len(dims))])
    return gain


def split_up(number_of, total, bound, skew):
    loads = [(1 << 20) // math.isqrt(rank ** skew) + 1 for rank in range(2, number_of + 1)]
    spare, given = total - bound - (number_of - 1), [1] * (number_of - 1)
    while spare > 0:
        free = [i for i in range(number_of - 1) if given[i] < bound]
        pool, budget = sum([loads[i] for i in free]), spare
        for i in free:
            more = min(bound - given[i], max(1, budget * loads[i] // pool), spare)
            given[i] = given[i] + more
            spare = spare - more
    return np.array([bound] + given)


def uneven_parts(own_key, count, total, limit, slope):
    if count == 2:
        one = jax.random.randint(own_key, (), max(1, total - limit), min(limit, total - 1) + 1)
        return jnp.stack([one, total - one])
    lengths = jnp.asarray(split_up(count, total, limit, slope), jnp.int32)
    twos = (count - 1) // 2
    donor, receiver = lengths[1:1 + 2 * twos:2], lengths[2:2 + 2 * twos:2]
    room = jnp.minimum(donor - 1, limit - receiver)
    passed = jax.random.randint(jax.random.fold_in(own_key, 1), (twos,), 0, 1 << 20) % (room + 1)
    lengths = lengths.at[1:1 + 2 * twos:2].set(donor - passed).at[2:2 + 2 * twos:2].set(receiver + passed)
    return lengths[jax.random.permutation(jax.random.fold_in(own_key, 2), count)]


def scatter_about(rng, shape, spread, limit, cuts=(), kind=jnp.bfloat16):
    array = spread * jax.random.normal(rng, shape, jnp.float32)
    if cuts:
        array = array * steps_of(rng, shape, cuts, -0.22, 0.18)
    return jnp.clip(array, -limit, limit).astype(kind)


def setup_inputs(seed: int = 0, part: int = 0) -> dict:
    keys = jax.random.split(jax.random.key(seed), 14)
    part_splits = jax.random.split(jax.random.fold_in(keys[13], part), 14)
    return {
        "x_in": scatter_about(part_splits[0], (TOKENS, INNER), 1.0, 6.0, ((0, 16), (1, 8))),
        "bc_in": scatter_about(part_splits[1], (TOKENS, GROUPS, 2 * STATE), 1.0, 6.0, ((0, 16), (1, 8))),
        "dt_in": draw_dt_in(jax.random.fold_in(jax.random.fold_in(keys[13], part), 71), part),
        "conv_x": scatter_about(keys[3], (CONV, INNER), 0.5, 3.0, ((1, 8),), jnp.float32),
        "conv_bc": scatter_about(keys[4], (CONV, GROUPS, 2 * STATE), 0.5, 3.0, ((1, 8),), jnp.float32),
        "a_log": draw_a_log(jax.random.fold_in(keys[13], 71), part),
        "dt_bias": jnp.clip(jax.random.uniform(keys[6], (HEADS,), jnp.float32, -1.0, 1.0) * steps_of(keys[6], (HEADS,), ((0, 8),), -0.4, 0.0), -1.0, 1.0),
        "d_skip": jnp.clip(0.5 + 1.0 * jax.random.uniform(keys[7], (HEADS,), jnp.float32) ** steps_of(keys[7], (HEADS,), ((0, 8),), -0.2, 0.2), 0.5, 1.5),
        "norm_gain": jnp.clip(1.0 + 0.1 * jax.random.normal(keys[8], (INNER,), jnp.float32), 0.5, 1.5),
        "doc_lengths": uneven_parts(part_splits[9], DOCS, TOKENS, TOKENS * 3 // 4, 2).astype(jnp.int32),
        "dec_x": scatter_about(part_splits[10], (CONTINUATIONS_N, STEPS, INNER), 1.0, 6.0, ((0, 16), (2, 8))),
        "dec_bc": scatter_about(part_splits[11], (CONTINUATIONS_N, STEPS, GROUPS, 2 * STATE), 1.0, 6.0, ((0, 16), (2, 8))),
        "dec_dt": scatter_about(part_splits[12], (CONTINUATIONS_N, STEPS, HEADS), 1.0, 5.0, ((0, 16), (2, 8)), jnp.float32),
    }


epsilon = 1e-05

def seg_of(doc_lengths, positions):
    doc_ends = jnp.cumsum(doc_lengths).astype(jnp.int32)
    counted = lax.optimization_barrier(jnp.sum((positions[:, None] >= doc_ends[None, :]).astype(jnp.int32), axis=1)).astype(jnp.int32)
    return jnp.where(positions < 0, jnp.int32(-1), counted).astype(jnp.int32)

def conv_silu(extended, ext_seg, taps):
    tok_count = extended.shape[0] - CONV + 1
    mine_seg = ext_seg[CONV - 1:]
    totals = jnp.zeros((tok_count,) + extended.shape[1:], jnp.float32)
    for tap_index in range(CONV):
        same_doc = (ext_seg[tap_index:tap_index + tok_count] == mine_seg).astype(jnp.float32)
        same_doc = same_doc.reshape((tok_count,) + (1,) * (extended.ndim - 1))
        totals = totals + taps[tap_index] * extended[tap_index:tap_index + tok_count].astype(jnp.float32) * same_doc
    return jax.nn.silu(totals).astype(jnp.bfloat16)

def block_terms(x_block, bc_block, dt_block, linear_attention_block, seg_block, seg_before, d_skip):
    tok_count, heads_here, head_width = x_block.shape
    groups_here = bc_block.shape[1]
    per_group = heads_here // groups_here
    state_size = bc_block.shape[2] // 2
    b_part = bc_block[:, :, :state_size].astype(jnp.float32)
    readout_part = bc_block[:, :, state_size:].astype(jnp.float32)
    input_split = x_block.astype(jnp.float32).reshape(tok_count, groups_here, per_group, head_width)
    cumul = jnp.cumsum(linear_attention_block, axis=0)
    positions_in = jnp.arange(tok_count)
    allowed = (positions_in[:, None] >= positions_in[None, :]) & (seg_block[:, None] == seg_block[None, :])
    scores = jnp.einsum('tgn,sgn->gts', readout_part, b_part)
    cumul_split = cumul.T.reshape(groups_here, per_group, tok_count)
    cum_gaps = cumul_split[:, :, :, None] - cumul_split[:, :, None, :]
    decay_factors = jnp.exp(jnp.where(allowed[None, None], cum_gaps, -jnp.inf))
    dt_split = dt_block.T.reshape(groups_here, per_group, tok_count)
    mixing_matrix = (scores[:, None] * decay_factors * dt_split[:, :, None, :]).astype(jnp.bfloat16)
    inner_piece = jnp.einsum('kaew,wkal->ekal', mixing_matrix.astype(jnp.float32), input_split)
    last_cum = cumul[-1]
    same_end = (seg_block == seg_block[-1]).astype(jnp.float32)
    inflow_scale = jnp.exp(last_cum[None, :] - cumul) * same_end[:, None] * dt_block
    inflow = (b_part[:, :, None, :] * inflow_scale.reshape(tok_count, groups_here, per_group)[:, :, :, None]).astype(jnp.bfloat16)
    block_state = jnp.einsum('sgrp,sgrn->grpn', input_split, inflow.astype(jnp.float32)).reshape(heads_here, head_width, state_size)
    through = jnp.exp(last_cum) * (seg_block[-1] == seg_before).astype(jnp.float32)
    keep_factor = jnp.exp(cumul) * (seg_block == seg_before).astype(jnp.float32)[:, None]
    local_part = inner_piece.reshape(tok_count, heads_here, head_width) + d_skip[None, :, None] * x_block.astype(jnp.float32)
    return (local_part, keep_factor, through, block_state)

def carried_part(bc_block, state_in, keep_factor):
    tok_count, groups_here, doubled = bc_block.shape
    state_size = doubled // 2
    heads_here, head_width, state_dim = state_in.shape
    readout_part = bc_block[:, :, state_size:].astype(jnp.float32)
    rounded = lax.optimization_barrier(state_in.astype(jnp.bfloat16)).astype(jnp.float32)
    rounded = rounded.reshape(groups_here, heads_here // groups_here, head_width, state_dim)
    result = jnp.einsum('tgn,grpn->tgrp', readout_part, rounded).reshape(tok_count, heads_here, head_width)
    return result * keep_factor[:, :, None]

def group_norm(raw_out, norm_gain, groups_here):
    tok_count = raw_out.shape[0]
    grouped = raw_out.reshape(tok_count, groups_here, -1)
    scaling = lax.rsqrt(lax.optimization_barrier(jnp.mean(grouped * grouped, axis=-1, keepdims=True)) + epsilon)
    return ((grouped * scaling).reshape(tok_count, -1) * norm_gain).astype(jnp.bfloat16)

def decode_one(tail_x, tail_bc, tail_seg, last_seg, dec_x, dec_bc, dec_dt, start_state, conv_x, conv_bc, a_log, dt_bias, d_skip, norm_gain):
    step_count = dec_x.shape[0]
    ext_seg = jnp.concatenate([tail_seg, jnp.full((step_count,), last_seg, jnp.int32)]).astype(jnp.int32)
    x_steps = conv_silu(jnp.concatenate([tail_x, dec_x]), ext_seg, conv_x)
    bc_steps = conv_silu(jnp.concatenate([tail_bc, dec_bc]), ext_seg, conv_bc)
    heads_here, head_width, state_size = start_state.shape
    groups_here = bc_steps.shape[1]
    per_group = heads_here // groups_here
    step_dt = jax.nn.softplus(dec_dt + dt_bias)
    step_decay = jnp.exp(-step_dt * jnp.exp(a_log))
    current = start_state.reshape(groups_here, per_group, head_width, state_size)
    outputs = []
    for step_index in range(step_count):
        x_now = x_steps[step_index].astype(jnp.float32).reshape(groups_here, per_group, head_width)
        b_now = bc_steps[step_index, :, :state_size].astype(jnp.float32)
        c_now = bc_steps[step_index, :, state_size:].astype(jnp.float32)
        decay_now = step_decay[step_index].reshape(groups_here, per_group)
        dt_now = step_dt[step_index].reshape(groups_here, per_group)
        current = decay_now[:, :, None, None] * current + (dt_now[:, :, None] * x_now)[:, :, :, None] * b_now[:, None, None, :]
        reading = jnp.einsum('grpn,gn->grp', current, c_now, precision=lax.Precision.HIGHEST)
        reading = reading + d_skip.reshape(groups_here, per_group)[:, :, None] * x_now
        outputs.append(reading.reshape(heads_here, head_width))
    return group_norm(jnp.stack(outputs), norm_gain, groups_here)

def reference(x_in, bc_in, dt_in, conv_x, conv_bc, a_log, dt_bias, d_skip, norm_gain, doc_lengths, dec_x, dec_bc, dec_dt):
    tok_total = x_in.shape[0]
    reach = CONV - 1
    ext_pos = jnp.arange(tok_total + reach, dtype=jnp.int32) - reach
    ext_seg = seg_of(doc_lengths, ext_pos)
    x_conv = conv_silu(jnp.concatenate([jnp.zeros((reach, INNER), jnp.bfloat16), x_in]), ext_seg, conv_x)
    bc_conv = conv_silu(jnp.concatenate([jnp.zeros((reach, GROUPS, 2 * STATE), jnp.bfloat16), bc_in]), ext_seg, conv_bc)
    step_dt = jax.nn.softplus(dt_in + dt_bias)
    log_decay = -step_dt * jnp.exp(a_log)
    tok_seg = ext_seg[reach:]
    block_count = tok_total // BLOCK
    before_seg = ext_seg[reach - 1 + jnp.arange(block_count) * BLOCK]
    blocks = (x_conv.reshape(block_count, BLOCK, HEADS, HEAD_DIM), bc_conv.reshape(block_count, BLOCK, GROUPS, 2 * STATE), step_dt.reshape(block_count, BLOCK, HEADS), log_decay.reshape(block_count, BLOCK, HEADS), tok_seg.reshape(block_count, BLOCK), before_seg)

    def advance(state_in, block):
        x_block, bc_block, dt_block, linear_attention_block, seg_block, seg_before = block
        local_part, keep_factor, through, block_state = block_terms(x_block, bc_block, dt_block, linear_attention_block, seg_block, seg_before, d_skip)
        result = local_part + carried_part(bc_block, state_in, keep_factor)
        return (through[:, None, None] * state_in + block_state, result)
    final_state, raw_blocks = lax.scan(advance, jnp.zeros((HEADS, HEAD_DIM, STATE), jnp.float32), blocks)
    prompt_out = group_norm(raw_blocks.reshape(tok_total, HEADS, HEAD_DIM), norm_gain, GROUPS)
    tail_seg = ext_seg[tok_total:]
    tail_x = x_in[tok_total - reach:]
    tail_bc = bc_in[tok_total - reach:]
    last_seg = DOCS - 1

    def sample(one_x, one_bc, one_dt):
        return decode_one(tail_x, tail_bc, tail_seg, last_seg, one_x, one_bc, one_dt, final_state, conv_x, conv_bc, a_log, dt_bias, d_skip, norm_gain)
    decode_out = jax.vmap(sample)(dec_x, dec_bc, dec_dt)
    return (prompt_out, decode_out)
```

```python
import functools

import jax
import jax.numpy as jnp
from jax import lax
from jax.experimental import pallas as pl
from jax.experimental.pallas import tpu as pltpu
from jax.sharding import PartitionSpec as P

BLOCK = 256
TILE = 128
HALO = 16
EPSILON = 1e-05
LOG2E = 1.4426950408889634
MESH = pl.DeviceIdType.MESH
F32 = jnp.float32
BF16 = jnp.bfloat16


def dot(a, b):
    return jnp.dot(a, b, preferred_element_type=F32)


def split3(value):
    high = value.astype(BF16).astype(F32)
    rest = value - high
    middle = rest.astype(BF16).astype(F32)
    low = (rest - middle).astype(BF16).astype(F32)
    return [high, middle, low]


def softplus(value):
    return jnp.maximum(value, 0.0) + jnp.log1p(jnp.exp(-jnp.abs(value)))


def silu(value):
    half = 0.5 * value
    return half + half * jnp.tanh(half)


def conv_chain(rows, taps, linked):
    total = taps[0] * rows
    for tap in taps[1:]:
        total = tap * rows + linked * pltpu.roll(total, 1, 0)
    return total


def kernel(
    seq,
    x_hbm, bc_hbm, dt_hbm, conv_x_hbm, conv_bc_hbm, a_log_hbm, dt_bias_hbm, d_skip_hbm, gain_hbm, doc_hbm,
    dec_x_hbm, dec_bc_hbm, dec_dt_hbm,
    out_hbm, dec_out,
    conv_x, conv_bc, a_log, dt_bias, d_skip, gain, doc, dec_x, dec_bc, dec_dt,
    xbuf, bcbuf, dtbuf, tail_x, tail_bc, xs, xw, bs, cs, bst, expand_a, expand_b, colf, colb, keepb,
    vrow, vecs, part, enter_q, p_msg, p_recv, s_out, s_in, c_msg, c_recv, y_msg, y_recv,
    local, keepx, scm, small, obuf, dec_keep, dec_local,
    few_sem, load_sem, rim_ss, rim_rs, tail_ss, tail_rs, p_ss, p_rs, c_ss, c_rs, s_ss, s_rs, y_ss, y_rs, out_sem,
):
    me = lax.axis_index("seq")
    rows, inner = xs.shape
    blocks = rows // BLOCK
    heads = dtbuf.shape[0]
    width = inner // heads
    pairs = inner // TILE
    state = bs.shape[1]
    docs = doc.shape[0]
    total_rows = rows * seq
    last = seq - 1

    def peer(step):
        return lax.rem(me + step, seq)

    few = [
        (doc_hbm, doc),
        (a_log_hbm, a_log),
        (dt_bias_hbm, dt_bias),
        (d_skip_hbm, d_skip),
        (dt_hbm, dtbuf),
        (conv_x_hbm, conv_x),
        (conv_bc_hbm, conv_bc),
        (gain_hbm, gain),
        (dec_x_hbm, dec_x),
        (dec_bc_hbm, dec_bc),
        (dec_dt_hbm, dec_dt),
    ]
    few = [pltpu.make_async_copy(far, near, few_sem.at[i]) for i, (far, near) in enumerate(few)]
    for copy in few:
        copy.start()
    loads = []
    for b in reversed(range(blocks)):
        there, here = pl.ds(b * BLOCK, BLOCK), pl.ds(HALO + b * BLOCK, BLOCK)
        loads.append(
            (
                pltpu.make_async_copy(x_hbm.at[there], xbuf.at[here], load_sem.at[2 * b]),
                pltpu.make_async_copy(bc_hbm.at[there], bcbuf.at[here], load_sem.at[2 * b + 1]),
            )
        )
        for copy in loads[-1]:
            copy.start()

    barrier = pltpu.get_barrier_semaphore()

    def greet(step, carry):
        pl.semaphore_signal(barrier, inc=1, device_id={"seq": peer(step)}, device_id_type=MESH)
        return carry

    lax.fori_loop(1, seq, greet, 0)

    few[0].wait()
    ends = []
    running = jnp.int32(0)
    for i in range(docs):
        running = running + doc[i]
        ends.append(running)
    base = me * rows

    def start_of(position):
        found = jnp.int32(0)
        for end in ends:
            found = jnp.where(end <= position, jnp.maximum(found, end), found)
        return found

    def next_after(position):
        found = jnp.where(position < 0, jnp.int32(0), jnp.int32(2 * total_rows))
        for end in ends:
            found = jnp.where(end > position, jnp.minimum(found, end), found)
        return found

    def linked_of(positions):
        linked = positions != 0
        for end in ends:
            linked = linked & (positions != end)
        return linked.astype(F32)

    head_row = lax.broadcasted_iota(jnp.int32, (TILE, inner), 0)
    head_of = lax.broadcasted_iota(jnp.int32, (TILE, inner), 1) // width
    expand_a[...] = ((head_row < 3 * heads) & (lax.rem(head_row, heads) == head_of)).astype(BF16)
    expand_b[...] = (
        (head_row >= 3 * heads) & (head_row < 6 * heads) & (lax.rem(head_row, heads) == head_of)
    ).astype(BF16)
    upper = (
        lax.broadcasted_iota(jnp.int32, (BLOCK, BLOCK), 0)
        <= lax.broadcasted_iota(jnp.int32, (BLOCK, BLOCK), 1)
    ).astype(BF16)
    lane = lax.broadcasted_iota(jnp.int32, (heads, TILE), 1)

    for copy in few[1:5]:
        copy.wait()
    small[...] = jnp.zeros_like(small)
    small[0:1, 0:heads] = a_log[...]
    small[1:2, 0:heads] = dt_bias[...]
    small[2:3, 0:heads] = d_skip[...]
    columns = small[...].T
    rate = jnp.exp(columns[0:heads, 0:1]) * LOG2E
    bias = columns[0:heads, 1:2]
    skip = columns[0:heads, 2:3]

    steps = [softplus(dtbuf[:, b * BLOCK : (b + 1) * BLOCK] + bias) for b in range(blocks)]
    parts = []
    for step in steps:
        parts += split3(-step * rate)
    sums = dot(jnp.concatenate(parts, axis=0).astype(BF16), upper)
    before = jnp.zeros((heads, 1), F32)
    whole = jnp.ones((heads, 1), F32)
    throughs = []
    dev_next = next_after(base - 1)
    for b in range(blocks):
        at = 3 * b * heads
        cum = sums[at : at + heads] + sums[at + heads : at + 2 * heads] + sums[at + 2 * heads : at + 3 * heads]
        step = steps[b]
        first = base + b * BLOCK
        end = first + BLOCK - 1
        position = first + lax.broadcasted_iota(jnp.int32, (heads, BLOCK), 1)
        cum_end = cum[:, BLOCK - 1 : BLOCK]
        inflow = jnp.where(position >= start_of(end), jnp.exp2(cum_end - cum) * step, 0.0)
        keep_dev = jnp.where(position < dev_next, jnp.exp2(cum + before), 0.0)
        table = jnp.concatenate(
            split3(inflow) + split3(keep_dev) + [cum, jnp.zeros((TILE - 7 * heads, BLOCK), F32)], axis=0
        ).T
        here = pl.ds(b * BLOCK, BLOCK)
        colf[here] = table
        colb[here] = table.astype(BF16)
        vrow[b] = cum - jnp.log2(step)
        block_next = next_after(first - 1)
        if b:
            keep = jnp.where(position < block_next, jnp.exp2(cum), 0.0)
            keepb[b - 1] = (
                jnp.concatenate(split3(keep) + [jnp.zeros((TILE - 3 * heads, BLOCK), F32)], axis=0)
                .T.astype(BF16)
            )
        throughs.append(jnp.where(end < block_next, jnp.exp2(cum_end), 0.0))
        before = before + cum_end
    whole = jnp.where(base + rows - 1 < dev_next, jnp.exp2(before), 0.0)
    picked = jnp.zeros((heads, TILE), F32)
    for i, column in enumerate([whole, skip] + throughs):
        picked = jnp.where(lane == i, column, picked)
    picked = jnp.concatenate(split3(picked) + [jnp.zeros((TILE - 3 * heads, TILE), F32)], axis=0)
    vecs[...] = dot(picked.T.astype(BF16), expand_a[...])[0:8]

    for copy in few[5:]:
        copy.wait()
    for copy in loads[0]:
        copy.wait()
    pl.semaphore_wait(barrier, seq - 1)
    edge = pl.ds(rows, HALO)

    def rim_copies(to):
        return [
            pltpu.make_async_remote_copy(
                src_ref=buf.at[edge], dst_ref=buf.at[pl.ds(0, HALO)], send_sem=rim_ss.at[i],
                recv_sem=rim_rs.at[i], device_id={"seq": to}, device_id_type=MESH,
            )
            for i, buf in enumerate((xbuf, bcbuf))
        ]

    def tail_copies(to):
        return [
            pltpu.make_async_remote_copy(
                src_ref=buf.at[edge], dst_ref=tail, send_sem=tail_ss.at[i, to],
                recv_sem=tail_rs.at[i], device_id={"seq": to}, device_id_type=MESH,
            )
            for i, (buf, tail) in enumerate(((xbuf, tail_x), (bcbuf, tail_bc)))
        ]

    @pl.when(me < last)
    def _():
        for copy in rim_copies(me + 1):
            copy.start()

    @pl.when(me == last)
    def _():
        def send(to, carry):
            for copy in tail_copies(to):
                copy.start()
            return carry

        lax.fori_loop(0, last, send, 0)
        tail_x[...] = xbuf[edge]
        tail_bc[...] = bcbuf[edge]

    @pl.when(me == 0)
    def _():
        xbuf[pl.ds(0, HALO)] = jnp.zeros((HALO, inner), BF16)
        bcbuf[pl.ds(0, HALO)] = jnp.zeros((HALO, 2 * state), BF16)

    def linked_rows(row):
        positions = base + row - 8 + lax.broadcasted_iota(jnp.int32, (TILE + 8, TILE), 0)
        return linked_of(positions)

    def conv_tile(buf, taps, row, at, linked):
        lanes = slice(at, at + TILE)
        raw = buf[pl.ds(row, TILE + HALO), lanes].astype(F32)[HALO - 8 :]
        return silu(conv_chain(raw, [tap[:, lanes] for tap in taps], linked)[8:]).astype(BF16)

    x_taps = [conv_x[k : k + 1, :] for k in range(4)]
    bc_taps = [conv_bc[k] for k in range(4)]

    def conv_rows(row):
        here = pl.ds(row, TILE)
        linked = linked_rows(row)
        scales = colb[here]
        for p in range(pairs):
            lanes = slice(p * TILE, (p + 1) * TILE)
            value = conv_tile(xbuf, x_taps, row, p * TILE, linked)
            xs[here, lanes] = value
            xw[here, lanes] = (value.astype(F32) * dot(scales, expand_a[:, lanes])).astype(BF16)
        for at in range(0, state, TILE):
            value = conv_tile(bcbuf, bc_taps, row, at, linked)
            bs[here, at : at + TILE] = value
            bst[at : at + TILE, here] = value.astype(F32).T.astype(BF16)

    def conv_c_rows(row):
        here = pl.ds(row, TILE)
        linked = linked_rows(row)
        for at in range(0, state, TILE):
            cs[here, at : at + TILE] = conv_tile(bcbuf, bc_taps, row, state + at, linked)

    def block_part(b):
        here = pl.ds(b * BLOCK, BLOCK)
        for at in range(0, inner, 256):
            part[b, :, at : at + 256] = dot(bst[:, here], xw[here, at : at + 256])

    for b in reversed(range(blocks)):
        if b:
            for copy in loads[blocks - b]:
                copy.wait()
        else:

            @pl.when(me > 0)
            def _():
                for copy in rim_copies(me):
                    copy.wait_recv()

        for row in range(b * BLOCK, (b + 1) * BLOCK, TILE):
            conv_rows(row)
        block_part(b)

    decays = jnp.concatenate(split3(vecs[0:1, :]) + [jnp.zeros((HALO - 3, inner), F32)], axis=0).astype(BF16)
    for p in range(pairs):
        lanes = slice(p * TILE, (p + 1) * TILE)
        value = part[0, :, lanes]
        for b in range(1, blocks):
            enter_q[b - 1, :, lanes] = value.astype(BF16)
            value = vecs[2 + b : 3 + b, lanes] * value + part[b, :, lanes]
        value = value.astype(BF16)
        for half in range(2):
            p_msg[2 * p + half, 0:TILE] = value[half * TILE : (half + 1) * TILE]
            p_msg[2 * p + half, TILE:] = decays[:, lanes]

    def p_copy(step, to):
        return pltpu.make_async_remote_copy(
            src_ref=p_msg.at[to], dst_ref=p_recv.at[me], send_sem=p_ss.at[step],
            recv_sem=p_rs.at[step], device_id={"seq": to}, device_id_type=MESH,
        )

    def c_copy(step, to):
        return pltpu.make_async_remote_copy(
            src_ref=c_msg.at[lax.rem(to, 2)], dst_ref=c_recv.at[me], send_sem=c_ss.at[step],
            recv_sem=c_rs.at[step], device_id={"seq": to}, device_id_type=MESH,
        )

    def s_copy(step, to):
        return pltpu.make_async_remote_copy(
            src_ref=s_out.at[to], dst_ref=s_in.at[me], send_sem=s_ss.at[step],
            recv_sem=s_rs.at[step], device_id={"seq": to}, device_id_type=MESH,
        )

    def y_copy(step, to):
        return pltpu.make_async_remote_copy(
            src_ref=y_msg.at[to], dst_ref=y_recv.at[me], send_sem=y_ss.at[step],
            recv_sem=y_rs.at[step], device_id={"seq": to}, device_id_type=MESH,
        )

    def every(action):
        def body(step, carry):
            action(step, peer(step))
            return carry

        lax.fori_loop(1, seq, body, 0)

    every(lambda step, to: p_copy(step, to).start())
    p_recv[me] = p_msg[me]

    @pl.when(me != last)
    def _():
        for copy in tail_copies(me):
            copy.wait_recv()

    offsets = lax.broadcasted_iota(jnp.int32, (16, TILE), 0)
    tail_doc = jnp.int32(0)
    for end in ends:
        tail_doc = tail_doc + (end <= total_rows - 1).astype(jnp.int32)
    joined = (tail_doc == docs - 1).astype(F32)
    dec_linked = jnp.where(
        offsets < 8, linked_of(total_rows - 8 + offsets), jnp.where(offsets == 8, joined, 1.0)
    )

    def dec_conv(tail, given, taps, at):
        lanes = slice(at, at + TILE)
        ext = jnp.concatenate([tail[:, lanes].astype(F32)[8:], given[:, lanes].astype(F32)], axis=0)
        return silu(conv_chain(ext, [tap[:, lanes] for tap in taps], dec_linked)[8:]).astype(BF16).astype(F32)

    dec_bcs = [dec_conv(tail_bc, dec_bc, bc_taps, at) for at in range(0, 2 * state, TILE)]
    for i in range(2):
        c_msg[i] = jnp.concatenate([dec_bcs[2 + i], jnp.zeros((8, TILE), F32)], axis=0).astype(BF16)
    every(lambda step, to: c_copy(step, to).start())
    c_recv[me] = c_msg[lax.rem(me, 2)]

    def lane_dot(a, b):
        return lax.dot_general(a, b, (((1,), (1,)), ((), ())), preferred_element_type=F32)

    dec_c = jnp.concatenate(dec_bcs[2:], axis=1).astype(BF16)
    dec_b = jnp.concatenate(dec_bcs[:2], axis=1).astype(BF16)
    dec_scores = lane_dot(dec_c, dec_b)
    dec_step = softplus(dec_dt[...] + dt_bias[...])
    dec_cum = -dec_step * jnp.exp(a_log[...])
    dec_row = lax.broadcasted_iota(jnp.int32, (8, heads), 0)
    for shift in (1, 2, 4):
        dec_cum = dec_cum + jnp.where(dec_row >= shift, pltpu.roll(dec_cum, shift, 0), 0.0)
    factors = []
    for s in range(8):
        gap = jnp.where(dec_row >= s, dec_cum - dec_cum[s : s + 1], 0.0)
        weight = dec_scores[:, s : s + 1] * jnp.exp(gap) * dec_step[s : s + 1]
        factors.append(jnp.where(dec_row >= s, weight, 0.0))
    factors.append(jnp.exp(dec_cum))
    factors = jnp.concatenate(factors, axis=0)
    factors = jnp.concatenate(
        split3(factors) + [jnp.zeros((factors.shape[0], TILE - 3 * heads), F32)], axis=1
    ).astype(BF16)
    for p in range(pairs):
        lanes = slice(p * TILE, (p + 1) * TILE)
        wide = dot(factors, expand_a[:, lanes])
        given = dec_conv(tail_x, dec_x, x_taps, p * TILE)
        answer = vecs[1:2, lanes] * given
        for s in range(8):
            answer = answer + wide[8 * s : 8 * s + 8] * given[s : s + 1]
        dec_local[:, lanes] = answer
        dec_keep[:, lanes] = wide[64:72]

    left_half = lax.broadcasted_iota(jnp.int32, (BLOCK, TILE), 1) < width

    def block_scores(b):
        here = pl.ds(b * BLOCK, BLOCK)
        row = lax.broadcasted_iota(jnp.int32, (BLOCK, BLOCK), 0)
        col = lax.broadcasted_iota(jnp.int32, (BLOCK, BLOCK), 1)
        first = base + b * BLOCK
        starts = jnp.zeros((BLOCK, BLOCK), jnp.int32)
        for end in ends:
            starts = jnp.where(row >= end - first, jnp.maximum(starts, end - first), starts)
        scm[...] = jnp.where((col <= row) & (col >= starts), dot(cs[here], bst[:, here]), 0.0)

    def block_local(b):
        here = pl.ds(b * BLOCK, BLOCK)
        block_scores(b)
        top, low = slice(0, TILE), slice(TILE, BLOCK)
        for p in range(pairs):
            lanes = slice(p * TILE, (p + 1) * TILE)
            value = xs[here, lanes]
            zero = jnp.zeros_like(value)
            sides = [jnp.where(left_half, value, zero), jnp.where(left_half, zero, value)]
            tops, lows = [], []
            for head in (2 * p, 2 * p + 1):
                cum_col = colf[here, 6 * heads + head : 6 * heads + head + 1]
                v = vrow[b, head : head + 1, :]
                gap = jnp.minimum(cum_col[top] - v[:, :TILE], 126.0)
                tops.append((scm[top, :TILE] * jnp.exp2(gap)).astype(BF16))
                gap = jnp.minimum(cum_col[low] - v, 126.0)
                lows.append((scm[low, :] * jnp.exp2(gap)).astype(BF16))
            inner_top = dot(
                jnp.concatenate(tops, axis=1), jnp.concatenate([side[top] for side in sides], axis=0)
            )
            inner_low = dot(jnp.concatenate(lows, axis=1), jnp.concatenate(sides, axis=0))
            answer = jnp.concatenate([inner_top, inner_low], axis=0) + vecs[1:2, lanes] * value.astype(F32)
            if b:
                carried = dot(cs[here], enter_q[b - 1, :, lanes])
                answer = answer + dot(keepb[b - 1], expand_a[:, lanes]) * carried
            local[here, lanes] = answer
            keepx[here, lanes] = dot(colb[here], expand_b[:, lanes])

    for row in range(0, rows, TILE):
        conv_c_rows(row)
    for b in range(blocks - 1):
        block_local(b)

    def scan(k, value):
        step = lax.rem(me - k + seq, seq)

        @pl.when(k != me)
        def _():
            p_copy(step, me).wait_recv()

        s_out[k] = value.astype(BF16)
        tags = p_recv[k, TILE:].astype(F32)
        decay = tags[0:1] + tags[1:2] + tags[2:3]
        return decay * value + p_recv[k, 0:TILE].astype(F32)

    final = lax.fori_loop(0, seq, scan, jnp.zeros((TILE, TILE), F32))
    every(lambda step, to: s_copy(step, to).start())
    s_in[me] = s_out[me]
    every(lambda step, to: c_copy(step, to).wait_recv())
    asked = c_recv[...].reshape(seq * 16, TILE)
    replies = sum(dot(asked, piece.astype(BF16)) for piece in split3(final))
    y_msg[...] = replies.reshape(seq, 16, TILE)[:, 0:8]
    every(lambda step, to: y_copy(step, to).start())
    y_recv[me] = y_msg[me]

    block_local(blocks - 1)

    def norm(pieces):
        squares = sum(piece * piece for piece in pieces)
        scale = lax.rsqrt(jnp.sum(squares, axis=1, keepdims=True) / inner + EPSILON)
        return [piece * scale for piece in pieces]

    every(lambda step, to: y_copy(step, to).wait_recv())
    pieces = []
    for p in range(pairs):
        lanes = slice(p * TILE, (p + 1) * TILE)
        pieces.append(dec_local[:, lanes] + dec_keep[:, lanes] * (y_recv[2 * p] + y_recv[2 * p + 1]))
    for p, piece in enumerate(norm(pieces)):
        lanes = slice(p * TILE, (p + 1) * TILE)
        dec_out[:, lanes] = (piece * gain[:, lanes]).astype(BF16)

    every(lambda step, to: s_copy(step, to).wait_recv())

    def finish(i, carry):
        row = pl.multiple_of(i * TILE, TILE)
        here = pl.ds(row, TILE)
        readout = cs[here]
        pieces = []
        for q in range(pairs // 2):
            entering = jnp.concatenate(
                [
                    jnp.concatenate([s_in[4 * q], s_in[4 * q + 1]], axis=0),
                    jnp.concatenate([s_in[4 * q + 2], s_in[4 * q + 3]], axis=0),
                ],
                axis=1,
            )
            lanes = slice(q * 256, (q + 1) * 256)
            pieces.append(local[here, lanes] + keepx[here, lanes] * dot(readout, entering))
        squares = sum(jnp.sum(piece * piece, axis=1, keepdims=True) for piece in pieces)
        scale = lax.rsqrt(squares / inner + EPSILON)
        for q, piece in enumerate(pieces):
            lanes = slice(q * 256, (q + 1) * 256)
            obuf[here, lanes] = (piece * scale * gain[:, lanes]).astype(BF16)
        pltpu.make_async_copy(obuf.at[here], out_hbm.at[here], out_sem.at[i]).start()
        return carry

    lax.fori_loop(0, rows // TILE, finish, 0)

    @pl.when(me < last)
    def _():
        for copy in rim_copies(me + 1):
            copy.wait_send()

    @pl.when(me == last)
    def _():
        def sent(to, carry):
            for copy in tail_copies(to):
                copy.wait_send()
            return carry

        lax.fori_loop(0, last, sent, 0)

    def settle(step, to):
        for copy in (p_copy, c_copy, s_copy, y_copy):
            copy(step, to).wait_send()

    every(settle)

    def written(i, carry):
        here = pl.ds(pl.multiple_of(i * TILE, TILE), TILE)
        pltpu.make_async_copy(obuf.at[here], out_hbm.at[here], out_sem.at[i]).wait()
        return carry

    lax.fori_loop(0, rows // TILE, written, 0)


def body(
    x_in, bc_in, dt_in, conv_x, conv_bc, a_log, dt_bias, d_skip, norm_gain, doc_lengths, dec_x, dec_bc, dec_dt
):
    rows, inner = x_in.shape
    heads = dt_in.shape[1]
    double = bc_in.shape[2]
    state = double // 2
    seq = lax.axis_size("seq")
    blocks = rows // BLOCK
    whole = pl.BlockSpec(memory_space=pl.ANY)
    near = pl.BlockSpec(memory_space=pltpu.VMEM)
    dma = pltpu.SemaphoreType.DMA
    vmem = pltpu.VMEM
    prompt, decoded = pl.pallas_call(
        functools.partial(kernel, seq),
        out_shape=(
            jax.ShapeDtypeStruct((rows, inner), BF16),
            jax.ShapeDtypeStruct((8, inner), BF16),
        ),
        in_specs=[whole] * 13,
        out_specs=(whole, near),
        scratch_shapes=[
            vmem(conv_x.shape, F32),
            vmem(conv_bc.shape, F32),
            vmem((1, heads), F32),
            vmem((1, heads), F32),
            vmem((1, heads), F32),
            vmem((1, inner), F32),
            pltpu.SMEM(doc_lengths.shape, jnp.int32),
            vmem((8, inner), BF16),
            vmem((8, double), BF16),
            vmem((8, heads), F32),
            vmem((HALO + rows, inner), BF16),
            vmem((HALO + rows, double), BF16),
            vmem((heads, rows), F32),
            vmem((HALO, inner), BF16),
            vmem((HALO, double), BF16),
            vmem((rows, inner), BF16),
            vmem((rows, inner), BF16),
            vmem((rows, state), BF16),
            vmem((rows, state), BF16),
            vmem((state, rows), BF16),
            vmem((TILE, inner), BF16),
            vmem((TILE, inner), BF16),
            vmem((rows, TILE), F32),
            vmem((rows, TILE), BF16),
            vmem((blocks - 1, BLOCK, TILE), BF16),
            vmem((blocks, heads, BLOCK), F32),
            vmem((8, inner), F32),
            vmem((blocks, state, inner), F32),
            vmem((blocks - 1, state, inner), BF16),
            vmem((seq, TILE + HALO, TILE), BF16),
            vmem((seq, TILE + HALO, TILE), BF16),
            vmem((seq, TILE, TILE), BF16),
            vmem((seq, TILE, TILE), BF16),
            vmem((2, 16, TILE), BF16),
            vmem((seq, 16, TILE), BF16),
            vmem((seq, 8, TILE), F32),
            vmem((seq, 8, TILE), F32),
            vmem((rows, inner), F32),
            vmem((rows, inner), F32),
            vmem((BLOCK, BLOCK), F32),
            vmem((TILE, TILE), F32),
            vmem((rows, inner), BF16),
            vmem((8, inner), F32),
            vmem((8, inner), F32),
            dma((11,)),
            dma((2 * blocks,)),
            dma((2,)),
            dma((2,)),
            dma((2, seq)),
            dma((2,)),
        ]
        + [dma((seq,))] * 8
        + [dma((rows // TILE,))],
        compiler_params=pltpu.CompilerParams(
            collective_id=0, has_side_effects=True, vmem_limit_bytes=60 << 20
        ),
    )(
        x_in,
        bc_in.reshape(rows, double),
        dt_in.T,
        conv_x,
        conv_bc,
        a_log.reshape(1, heads),
        dt_bias.reshape(1, heads),
        d_skip.reshape(1, heads),
        norm_gain.reshape(1, inner),
        doc_lengths,
        dec_x.reshape(8, inner),
        dec_bc.reshape(8, double),
        dec_dt.reshape(8, heads),
    )
    return prompt, decoded.reshape(1, 8, inner)


def solution(mesh):
    placed = (
        P(("group", "seq"), "head"),
        P(("group", "seq"), "head", None),
        P(("group", "seq"), "head"),
        P(None, "head"),
        P(None, "head", None),
        P("head"),
        P("head"),
        P("head"),
        P("head"),
        P("group"),
        P(("group", "seq"), None, "head"),
        P(("group", "seq"), None, "head", None),
        P(("group", "seq"), None, "head"),
    )
    return jax.shard_map(
        body,
        mesh=mesh,
        in_specs=placed,
        out_specs=(P(("group", "seq"), "head"), P(("group", "seq"), None, "head")),
        check_vma=False,
    )
```

```python
import functools

import jax
import jax.numpy as jnp
from jax import lax
from jax.experimental import pallas as pl
from jax.experimental.pallas import tpu as pltpu
from jax.sharding import PartitionSpec as P

BLOCK = 256
TILE = 128
HALO = 16
EPSILON = 1e-05
LOG2E = 1.4426950408889634
MESH = pl.DeviceIdType.MESH
F32 = jnp.float32
BF16 = jnp.bfloat16


def dot(a, b):
    return jnp.dot(a, b, preferred_element_type=F32)


def split3(value):
    high = value.astype(BF16).astype(F32)
    rest = value - high
    middle = rest.astype(BF16).astype(F32)
    low = (rest - middle).astype(BF16).astype(F32)
    return [high, middle, low]


def softplus(value):
    return jnp.maximum(value, 0.0) + jnp.log1p(jnp.exp(-jnp.abs(value)))


def silu(value):
    half = 0.5 * value
    return half + half * jnp.tanh(half)


def conv_chain(rows, taps, linked):
    total = taps[0] * rows
    for tap in taps[1:]:
        total = tap * rows + linked * pltpu.roll(total, 1, 0)
    return total


def kernel(
    seq,
    x_hbm, bc_hbm, dt_hbm, conv_x_hbm, conv_bc_hbm, a_log_hbm, dt_bias_hbm, d_skip_hbm, gain_hbm, doc_hbm,
    dec_x_hbm, dec_bc_hbm, dec_dt_hbm,
    out, dec_out,
    conv_x, conv_bc, a_log, dt_bias, d_skip, gain, doc, dec_x, dec_bc, dec_dt,
    xbuf, bcbuf, dtbuf, rim_msg, rim_recv, tail_recv, tail_f32, xs, xw, bs, cs, bst, expand_a, expand_b, colf, colb, keepb,
    vrow, vecs, enter_q, p_msg, p_recv, s_out, s_in,
    local, keepx, scm, small, edges, dec_factors, obuf, dec_keep, dec_local,
    few_sem, load_sem, rim_ss, rim_rs, tail_ss, tail_rs, p_ss, p_rs, s_ss, s_rs, out_sem,
):
    me = lax.axis_index("seq")
    rows, inner = xs.shape
    blocks = rows // BLOCK
    heads = dtbuf.shape[0]
    width = inner // heads
    pairs = inner // TILE
    state = bs.shape[1]
    docs = doc.shape[0]
    total_rows = rows * seq
    last = seq - 1

    def peer(step):
        return lax.rem(me + step, seq)

    few = [
        (doc_hbm, doc),
        (a_log_hbm, a_log),
        (dt_bias_hbm, dt_bias),
        (d_skip_hbm, d_skip),
        (dt_hbm, dtbuf),
        (conv_x_hbm, conv_x),
        (conv_bc_hbm, conv_bc),
        (gain_hbm, gain),
        (dec_x_hbm, dec_x),
        (dec_bc_hbm, dec_bc),
        (dec_dt_hbm, dec_dt),
    ]
    few = [pltpu.make_async_copy(far, near, few_sem.at[i]) for i, (far, near) in enumerate(few)]
    for copy in few:
        copy.start()
    loads = []
    for b in reversed(range(blocks)):
        there, here = pl.ds(b * BLOCK, BLOCK), pl.ds(HALO + b * BLOCK, BLOCK)
        loads.append(
            (
                pltpu.make_async_copy(x_hbm.at[there], xbuf.at[here], load_sem.at[2 * b]),
                pltpu.make_async_copy(bc_hbm.at[there], bcbuf.at[here], load_sem.at[2 * b + 1]),
            )
        )
        for copy in loads[-1]:
            copy.start()

    barrier = pltpu.get_barrier_semaphore()

    def greet(step, carry):
        pl.semaphore_signal(barrier, inc=1, device_id={"seq": peer(step)}, device_id_type=MESH)
        return carry

    lax.fori_loop(1, seq, greet, 0)

    few[0].wait()
    ends = []
    running = jnp.int32(0)
    for i in range(docs):
        running = running + doc[i]
        ends.append(running)
    base = me * rows

    def start_of(position):
        found = jnp.int32(0)
        for end in ends:
            found = jnp.where(end <= position, jnp.maximum(found, end), found)
        return found

    def next_after(position):
        found = jnp.where(position < 0, jnp.int32(0), jnp.int32(2 * total_rows))
        for end in ends:
            found = jnp.where(end > position, jnp.minimum(found, end), found)
        return found

    def linked_of(positions):
        linked = positions != 0
        for end in ends:
            linked = linked & (positions != end)
        return linked.astype(F32)

    head_row = lax.broadcasted_iota(jnp.int32, (TILE, inner), 0)
    channel = lax.broadcasted_iota(jnp.int32, (TILE, inner), 1)

    def spread(first):
        found = jnp.zeros((TILE, inner), jnp.bool_)
        for copy_at in range(first, first + 3 * heads, heads):
            low = (head_row - copy_at) * width
            found = found | ((channel >= low) & (channel < low + width) & (head_row >= copy_at))
        return found.astype(BF16)

    expand_a[...] = spread(0)
    expand_b[...] = spread(3 * heads)
    upper = (
        lax.broadcasted_iota(jnp.int32, (BLOCK, BLOCK), 0)
        <= lax.broadcasted_iota(jnp.int32, (BLOCK, BLOCK), 1)
    ).astype(BF16)
    lane = lax.broadcasted_iota(jnp.int32, (heads, TILE), 1)

    for copy in few[1:5]:
        copy.wait()
    small[...] = jnp.zeros_like(small)
    small[0:1, 0:heads] = a_log[...]
    small[1:2, 0:heads] = dt_bias[...]
    small[2:3, 0:heads] = d_skip[...]
    columns = small[...].T
    rate = jnp.exp(columns[0:heads, 0:1]) * LOG2E
    bias = columns[0:heads, 1:2]
    skip = columns[0:heads, 2:3]

    steps = [softplus(dtbuf[:, b * BLOCK : (b + 1) * BLOCK] + bias) for b in range(blocks)]
    parts = []
    for step in steps:
        parts += split3(-step * rate)
    sums = dot(jnp.concatenate(parts, axis=0).astype(BF16), upper)
    before = jnp.zeros((heads, 1), F32)
    whole = jnp.ones((heads, 1), F32)
    throughs = []
    dev_next = next_after(base - 1)
    for b in range(blocks):
        at = 3 * b * heads
        cum = sums[at : at + heads] + sums[at + heads : at + 2 * heads] + sums[at + 2 * heads : at + 3 * heads]
        step = steps[b]
        first = base + b * BLOCK
        end = first + BLOCK - 1
        position = first + lax.broadcasted_iota(jnp.int32, (heads, BLOCK), 1)
        cum_end = cum[:, BLOCK - 1 : BLOCK]
        inflow = jnp.where(position >= start_of(end), jnp.exp2(cum_end - cum) * step, 0.0)
        keep_dev = jnp.where(position < dev_next, jnp.exp2(cum + before), 0.0)
        table = jnp.concatenate(
            split3(inflow) + split3(keep_dev) + [cum, jnp.zeros((TILE - 7 * heads, BLOCK), F32)], axis=0
        ).T
        here = pl.ds(b * BLOCK, BLOCK)
        colf[here] = table
        colb[here] = table.astype(BF16)
        vrow[b] = cum - jnp.log2(step)
        block_next = next_after(first - 1)
        keep = jnp.where(position < block_next, jnp.exp2(cum), 0.0)
        keepb[b] = (
            jnp.concatenate(split3(keep) + [jnp.zeros((TILE - 3 * heads, BLOCK), F32)], axis=0)
            .T.astype(BF16)
        )
        throughs.append(jnp.where(end < block_next, jnp.exp2(cum_end), 0.0))
        before = before + cum_end
    whole = jnp.where(base + rows - 1 < dev_next, jnp.exp2(before), 0.0)
    picked = jnp.zeros((heads, TILE), F32)
    for i, column in enumerate([whole, skip] + throughs):
        picked = jnp.where(lane == i, column, picked)
    picked = jnp.concatenate(split3(picked) + [jnp.zeros((TILE - 3 * heads, TILE), F32)], axis=0)
    vecs[...] = dot(picked.T.astype(BF16), expand_a[...])[0:8]

    for copy in few[5:]:
        copy.wait()
    for copy in loads[0]:
        copy.wait()
    pl.semaphore_wait(barrier, seq - 1)
    edge = pl.ds(rows, HALO)
    pieces = []
    for buf, count in ((xbuf, inner // TILE), (bcbuf, 2 * state // TILE)):
        for t in range(count):
            pieces.append(buf[edge, t * TILE : (t + 1) * TILE].astype(F32)[HALO - 4 :])
    rim_msg[...] = jnp.concatenate(pieces, axis=0).astype(BF16)

    def rim_copy(to):
        return pltpu.make_async_remote_copy(
            src_ref=rim_msg, dst_ref=rim_recv, send_sem=rim_ss.at[0],
            recv_sem=rim_rs.at[0], device_id={"seq": to}, device_id_type=MESH,
        )

    def tail_copy(to):
        return pltpu.make_async_remote_copy(
            src_ref=rim_msg, dst_ref=tail_recv, send_sem=tail_ss.at[to],
            recv_sem=tail_rs.at[0], device_id={"seq": to}, device_id_type=MESH,
        )

    @pl.when(me < last)
    def _():
        rim_copy(me + 1).start()

    @pl.when(me == last)
    def _():
        def send(step, carry):
            tail_copy(last - step).start()
            return carry

        lax.fori_loop(1, seq, send, 0)
        tail_recv[...] = rim_msg[...]

    @pl.when(me == 0)
    def _():
        rim_recv[...] = jnp.zeros_like(rim_recv)

    def linked_rows(row):
        positions = base + row - 8 + lax.broadcasted_iota(jnp.int32, (TILE + 8, TILE), 0)
        return linked_of(positions)

    def conv_tile(buf, taps, row, at, linked):
        lanes = slice(at, at + TILE)
        raw = buf[pl.ds(row, TILE + HALO), lanes].astype(F32)[HALO - 8 :]
        return silu(conv_chain(raw, [tap(lanes) for tap in taps], linked)[8:]).astype(BF16)

    x_taps = [lambda lanes, k=k: conv_x[k : k + 1, lanes] for k in range(4)]
    bc_taps = [lambda lanes, k=k: conv_bc[k, :, lanes] for k in range(4)]

    def conv_rows(i, carry):
        row = pl.multiple_of((rows // TILE - 1 - i) * TILE, TILE)

        @pl.when((row == 0) & (me > 0))
        def _():
            rim_copy(me).wait_recv()

        @pl.when(row == 0)
        def _():
            rim = rim_recv[...].astype(F32)
            blank = jnp.zeros((HALO - 4, TILE), F32)
            at = 0
            for buf, count in ((xbuf, inner // TILE), (bcbuf, 2 * state // TILE)):
                for t in range(count):
                    piece = jnp.concatenate([blank, rim[at : at + 4]], axis=0)
                    buf[0:HALO, t * TILE : (t + 1) * TILE] = piece.astype(BF16)
                    at += 4

        here = pl.ds(row, TILE)
        linked = linked_rows(row)
        for at in range(0, state, TILE):
            value = conv_tile(bcbuf, bc_taps, row, at, linked)
            bs[here, at : at + TILE] = value
            bst[at : at + TILE, here] = value.astype(F32).T.astype(BF16)
        scales = colb[here]
        for p in range(pairs):
            lanes = slice(p * TILE, (p + 1) * TILE)
            value = conv_tile(xbuf, x_taps, row, p * TILE, linked)
            xs[here, lanes] = value
            xw[here, lanes] = (value.astype(F32) * dot(scales, expand_a[:, lanes])).astype(BF16)

        return carry

    def conv_c_rows(i, carry):
        row = pl.multiple_of(i * TILE, TILE)
        linked = linked_rows(row)
        for at in range(0, state, TILE):
            cs[pl.ds(row, TILE), at : at + TILE] = conv_tile(bcbuf, bc_taps, row, state + at, linked)
        return carry

    for pair in loads[1:]:
        for copy in pair:
            copy.wait()
    lax.fori_loop(0, rows // TILE, conv_rows, 0, unroll=2)

    offsets = lax.broadcasted_iota(jnp.int32, (16, TILE), 0)
    tail_doc = jnp.int32(0)
    for end in ends:
        tail_doc = tail_doc + (end <= total_rows - 1).astype(jnp.int32)
    joined = (tail_doc == docs - 1).astype(F32)
    dec_linked = jnp.where(
        offsets < 8, linked_of(total_rows - 8 + offsets), jnp.where(offsets == 8, joined, 1.0)
    )

    def dec_conv(tail_at, given, taps, at):
        lanes = pl.ds(at, TILE)
        ext = jnp.concatenate([tail_f32[pl.ds(tail_at, 8)], given[:, lanes].astype(F32)], axis=0)
        return silu(conv_chain(ext, [tap(lanes) for tap in taps], dec_linked)[8:]).astype(BF16).astype(F32)

    @pl.when(me != last)
    def _():
        tail_copy(me).wait_recv()

    tail = tail_recv[...].astype(F32)
    spaced = []
    for t in range(tail.shape[0] // 4):
        spaced += [jnp.zeros((4, TILE), F32), tail[4 * t : 4 * t + 4]]
    tail_f32[...] = jnp.concatenate(spaced, axis=0)
    dec_bcs = [dec_conv(8 * (pairs + at // TILE), dec_bc, bc_taps, at) for at in range(0, 2 * state, TILE)]

    def p_copy(part, step, to):
        return pltpu.make_async_remote_copy(
            src_ref=p_msg.at[part, to], dst_ref=p_recv.at[part, me], send_sem=p_ss.at[part, step],
            recv_sem=p_rs.at[part, step], device_id={"seq": to}, device_id_type=MESH,
        )

    def s_copy(part, step, to):
        return pltpu.make_async_remote_copy(
            src_ref=s_out.at[part, to], dst_ref=s_in.at[part, me], send_sem=s_ss.at[part, step],
            recv_sem=s_rs.at[part, step], device_id={"seq": to}, device_id_type=MESH,
        )

    def every(action):
        def body(step, carry):
            action(step, peer(step))
            return carry

        lax.fori_loop(1, seq, body, 0)

    edges[...] = jnp.concatenate(split3(vecs[0:1, :]) + [jnp.zeros((5, inner), F32)], axis=0)
    enter_q[0] = jnp.zeros((state, inner), BF16)
    share = state // 4

    def contribute(part):
        for g in range(part * pairs // 4, (part + 1) * pairs // 4):
            lanes = slice(g * BLOCK, (g + 1) * BLOCK)
            value = dot(bst[:, 0:BLOCK], xw[0:BLOCK, lanes])
            for b in range(1, blocks):
                here = slice(b * BLOCK, (b + 1) * BLOCK)
                enter_q[b, :, lanes] = value.astype(BF16)
                value = vecs[2 + b : 3 + b, lanes] * value + dot(bst[:, here], xw[here, lanes])
            value = value.astype(BF16)
            for p in range(2):
                decay = edges[:, g * BLOCK + p * TILE : g * BLOCK + (p + 1) * TILE]
                for quarter in range(4):
                    to = (8 * g + 4 * p + quarter) % seq
                    p_msg[part, to, 0:share] = value[quarter * share : (quarter + 1) * share, p * TILE : (p + 1) * TILE]
                    p_msg[part, to, share:] = jnp.concatenate([decay, dec_bcs[2 + quarter // 2]], axis=0).astype(BF16)

                    @pl.when(to != me)
                    def _(to=to):
                        p_copy(part, lax.rem(to - me + seq, seq), to).start()

        p_recv[part, me] = p_msg[part, me]

    contribute(0)
    contribute(1)
    lax.fori_loop(0, rows // TILE, conv_c_rows, 0, unroll=2)

    def lane_dot(a, b):
        return lax.dot_general(a, b, (((1,), (1,)), ((), ())), preferred_element_type=F32)

    dec_c = jnp.concatenate(dec_bcs[2:], axis=1).astype(BF16)
    dec_b = jnp.concatenate(dec_bcs[:2], axis=1).astype(BF16)
    dec_scores = lane_dot(dec_c, dec_b)
    dec_step = softplus(dec_dt[...] + dt_bias[...])
    dec_cum = -dec_step * jnp.exp(a_log[...])
    dec_row = lax.broadcasted_iota(jnp.int32, (8, heads), 0)
    for shift in (1, 2, 4):
        dec_cum = dec_cum + jnp.where(dec_row >= shift, pltpu.roll(dec_cum, shift, 0), 0.0)
    factors = []
    for s in range(8):
        gap = jnp.where(dec_row >= s, dec_cum - dec_cum[s : s + 1], 0.0)
        weight = dec_scores[:, s : s + 1] * jnp.exp(gap) * dec_step[s : s + 1]
        factors.append(jnp.where(dec_row >= s, weight, 0.0))
    factors.append(jnp.exp(dec_cum))
    factors = jnp.concatenate(factors, axis=0)
    factors = jnp.concatenate(
        split3(factors) + [jnp.zeros((factors.shape[0], TILE - 3 * heads), F32)], axis=1
    ).astype(BF16)
    dec_factors[...] = factors

    def given_pair(p, carry):
        at = pl.multiple_of(p * TILE, TILE)
        lanes = pl.ds(at, TILE)
        wide = dot(dec_factors[...], expand_a[:, lanes])
        given = dec_conv(pl.multiple_of(8 * p, 8), dec_x, x_taps, at)
        answer = vecs[1:2, lanes] * given
        for s in range(8):
            answer = answer + wide[8 * s : 8 * s + 8] * given[s : s + 1]
        dec_local[:, lanes] = answer
        dec_keep[:, lanes] = wide[64:72]
        return carry

    def given_tokens():
        lax.fori_loop(0, pairs, given_pair, 0)


    left_half = lax.broadcasted_iota(jnp.int32, (BLOCK, TILE), 1) < width

    def block_local(b, carry):
        here = pl.ds(pl.multiple_of(b * BLOCK, BLOCK), BLOCK)
        row = lax.broadcasted_iota(jnp.int32, (BLOCK, BLOCK), 0)
        col = lax.broadcasted_iota(jnp.int32, (BLOCK, BLOCK), 1)
        first = base + b * BLOCK
        starts = jnp.zeros((BLOCK, BLOCK), jnp.int32)
        for end in ends:
            starts = jnp.where(row >= end - first, jnp.maximum(starts, end - first), starts)
        scm[...] = jnp.where((col <= row) & (col >= starts), dot(cs[here], bst[:, here]), 0.0)
        top, low = slice(0, TILE), slice(TILE, BLOCK)

        for p in range(pairs):
            lanes = slice(p * TILE, (p + 1) * TILE)
            value = xs[here, lanes]
            zero = jnp.zeros_like(value)
            sides = [jnp.where(left_half, value, zero), jnp.where(left_half, zero, value)]
            tops, lows = [], []
            for side in range(2):
                head = 2 * p + side
                cum_col = colf[here, 6 * heads + head : 6 * heads + head + 1]
                v = vrow[b, head : head + 1, :]
                gap = jnp.minimum(cum_col[top] - v[:, :TILE], 126.0)
                tops.append((scm[top, :TILE] * jnp.exp2(gap)).astype(BF16))
                gap = jnp.minimum(cum_col[low] - v, 126.0)
                lows.append((scm[low, :] * jnp.exp2(gap)).astype(BF16))
            inner_top = dot(
                jnp.concatenate(tops, axis=1), jnp.concatenate([side[top] for side in sides], axis=0)
            )
            inner_low = dot(jnp.concatenate(lows, axis=1), jnp.concatenate(sides, axis=0))
            answer = jnp.concatenate([inner_top, inner_low], axis=0) + vecs[1:2, lanes] * value.astype(F32)
            carried = dot(cs[here], enter_q[b, :, lanes])
            local[here, lanes] = answer + dot(keepb[b], expand_a[:, lanes]) * carried
            keepx[here, lanes] = dot(colb[here], expand_b[:, lanes])
        return carry

    def answer(part):
        def scan(k, value):
            s_out[part, k, 0:share] = value.astype(BF16)
            tags = p_recv[part, k, share:].astype(F32)[0:8]
            decay = tags[0:1] + tags[1:2] + tags[2:3]
            return decay * value + p_recv[part, k, 0:share].astype(F32)

        every(lambda step, to: p_copy(part, step, me).wait_recv())
        final = lax.fori_loop(0, seq, scan, jnp.zeros((share, TILE), F32), unroll=8)
        even = lax.rem(me, 2) == 0
        zero = jnp.zeros_like(final)
        final = jnp.concatenate([jnp.where(even, final, zero), jnp.where(even, zero, final)], axis=0)
        asked = p_recv[part, :, share:].reshape(seq * HALO, TILE)
        replies = sum(dot(asked, piece.astype(BF16)) for piece in split3(final)[:2]).reshape(seq, HALO, TILE)[:, 8:]
        high = replies.astype(BF16).astype(F32)
        s_out[part, :, share:] = jnp.concatenate([high, replies - high], axis=1).astype(BF16)
        every(lambda step, to: s_copy(part, step, to).start())
        s_in[part, me] = s_out[part, me]

    lax.fori_loop(0, 1, block_local, 0)
    given_tokens()
    lax.fori_loop(1, blocks - 1, block_local, 0)
    answer(0)
    answer(1)
    lax.fori_loop(blocks - 1, blocks, block_local, 0)

    def carried_part(i, part):
        here = pl.ds(pl.multiple_of(i * TILE, TILE), TILE)
        readout = cs[here]
        pieces = []
        for g in range(pairs // 4):
            entering = jnp.concatenate(
                [
                    jnp.concatenate([s_in[part, 8 * g + 4 * p + t, 0:share] for t in range(4)], axis=0)
                    for p in range(2)
                ],
                axis=1,
            )
            at = part * inner // 2 + g * BLOCK
            lanes = slice(at, at + BLOCK)
            pieces.append(local[here, lanes] + keepx[here, lanes] * dot(readout, entering))
        squares = sum(piece * piece for piece in pieces)
        return here, pieces, squares[:, :TILE] + squares[:, TILE:]

    def finish_first(i, carry):
        here, pieces, squares = carried_part(i, 0)
        for g, piece in enumerate(pieces):
            local[here, g * BLOCK : (g + 1) * BLOCK] = piece
        colf[here] = squares
        return carry

    def finish(i, carry):
        here, pieces, squares = carried_part(i, 1)
        squares = jnp.sum(squares + colf[here], axis=1, keepdims=True)
        scale = lax.rsqrt(squares / inner + EPSILON)
        for g in range(pairs // 2):
            lanes = slice(g * BLOCK, (g + 1) * BLOCK)
            piece = local[here, lanes] if g < pairs // 4 else pieces[g - pairs // 4]
            obuf[here, lanes] = (piece * scale * gain[:, lanes]).astype(BF16)
        pltpu.make_async_copy(obuf.at[here], out.at[here], out_sem.at[i]).start()
        return carry

    every(lambda step, to: s_copy(0, step, to).wait_recv())
    lax.fori_loop(0, rows // TILE, finish_first, 0, unroll=2)
    every(lambda step, to: s_copy(1, step, to).wait_recv())
    lax.fori_loop(0, rows // TILE, finish, 0, unroll=2)

    def norm(pieces):
        squares = sum(piece * piece for piece in pieces)
        scale = lax.rsqrt(jnp.sum(squares, axis=1, keepdims=True) / inner + EPSILON)
        return [piece * scale for piece in pieces]

    pieces = []
    for p in range(pairs):
        lanes = slice(p * TILE, (p + 1) * TILE)
        part, first = 2 * p // pairs, 4 * p % seq
        tags = sum(s_in[part, first + t, share:].astype(F32) for t in range(4))
        pieces.append(dec_local[:, lanes] + dec_keep[:, lanes] * (tags[0:8] + tags[8:16]))
    for p, piece in enumerate(norm(pieces)):
        lanes = slice(p * TILE, (p + 1) * TILE)
        dec_out[:, lanes] = (piece * gain[:, lanes]).astype(BF16)

    @pl.when(me < last)
    def _():
        rim_copy(me + 1).wait_send()

    @pl.when(me == last)
    def _():
        def sent(to, carry):
            tail_copy(to).wait_send()
            return carry

        lax.fori_loop(0, last, sent, 0)

    def settle(step, to):
        for copy in (p_copy, s_copy):
            for part in range(2):
                copy(part, step, to).wait_send()

    every(settle)

    def written(i, carry):
        here = pl.ds(pl.multiple_of(i * TILE, TILE), TILE)
        pltpu.make_async_copy(obuf.at[here], out.at[here], out_sem.at[i]).wait()
        return carry

    lax.fori_loop(0, rows // TILE, written, 0)


def hand_over(held, held_dec, out, out_dec, buf, buf_dec, sem):
    rows = held.shape[0]
    count = sem.shape[1] - 1
    pairs = [((held_dec, buf_dec), (buf_dec, out_dec))]
    for i in range(count):
        here = pl.ds(i * rows // count, rows // count)
        pairs.append(((held.at[here], buf.at[here]), (buf.at[here], out.at[here])))
    copies = [
        [pltpu.make_async_copy(*move, sem.at[way, i]) for way, move in enumerate(moves)]
        for i, moves in enumerate(pairs)
    ]
    for come, _ in copies:
        come.start()
    for come, go in copies:
        come.wait()
        go.start()
    for _, go in copies:
        go.wait()


def body(
    x_in, bc_in, dt_in, conv_x, conv_bc, a_log, dt_bias, d_skip, norm_gain, doc_lengths, dec_x, dec_bc, dec_dt
):
    rows, inner = x_in.shape
    heads = dt_in.shape[1]
    double = bc_in.shape[2]
    state = double // 2
    seq = lax.axis_size("seq")
    blocks = rows // BLOCK
    edge_rows = 4 * (inner + double) // TILE
    whole = pl.BlockSpec(memory_space=pl.ANY)
    near = pl.BlockSpec(memory_space=pltpu.VMEM)
    dma = pltpu.SemaphoreType.DMA
    vmem = pltpu.VMEM
    prompt, decoded = pl.pallas_call(
        functools.partial(kernel, seq),
        out_shape=(
            jax.ShapeDtypeStruct((rows, inner), BF16),
            jax.ShapeDtypeStruct((8, inner), BF16),
        ),
        in_specs=[whole] * 13,
        out_specs=(whole, near),
        scratch_shapes=[
            vmem(conv_x.shape, F32),
            vmem(conv_bc.shape, F32),
            vmem((1, heads), F32),
            vmem((1, heads), F32),
            vmem((1, heads), F32),
            vmem((1, inner), F32),
            pltpu.SMEM(doc_lengths.shape, jnp.int32),
            vmem((8, inner), BF16),
            vmem((8, double), BF16),
            vmem((8, heads), F32),
            vmem((HALO + rows, inner), BF16),
            vmem((HALO + rows, double), BF16),
            vmem((heads, rows), F32),
            vmem((edge_rows, TILE), BF16),
            vmem((edge_rows, TILE), BF16),
            vmem((edge_rows, TILE), BF16),
            vmem((2 * edge_rows, TILE), F32),
            vmem((rows, inner), BF16),
            vmem((rows, inner), BF16),
            vmem((rows, state), BF16),
            vmem((rows, state), BF16),
            vmem((state, rows), BF16),
            vmem((TILE, inner), BF16),
            vmem((TILE, inner), BF16),
            vmem((rows, TILE), F32),
            vmem((rows, TILE), BF16),
            vmem((blocks, BLOCK, TILE), BF16),
            vmem((blocks, heads, BLOCK), F32),
            vmem((8, inner), F32),
            vmem((blocks, state, inner), BF16),
            vmem((2, seq, state // 4 + HALO, TILE), BF16),
            vmem((2, seq, state // 4 + HALO, TILE), BF16),
            vmem((2, seq, state // 4 + HALO, TILE), BF16),
            vmem((2, seq, state // 4 + HALO, TILE), BF16),
            vmem((rows, inner), F32),
            vmem((rows, inner), F32),
            vmem((BLOCK, BLOCK), F32),
            vmem((TILE, TILE), F32),
            vmem((8, inner), F32),
            vmem((72, TILE), BF16),
            vmem((rows, inner), BF16),
            vmem((8, inner), F32),
            vmem((8, inner), F32),
            dma((11,)),
            dma((2 * blocks,)),
            dma((1,)),
            dma((1,)),
            dma((seq,)),
            dma((1,)),
        ]
        + [dma((2, seq))] * 4
        + [dma((rows // TILE,))],
        compiler_params=pltpu.CompilerParams(
            collective_id=0, has_side_effects=True, vmem_limit_bytes=60 << 20
        ),
    )(
        x_in,
        bc_in.reshape(rows, double),
        dt_in.T,
        conv_x,
        conv_bc,
        a_log.reshape(1, heads),
        dt_bias.reshape(1, heads),
        d_skip.reshape(1, heads),
        norm_gain.reshape(1, inner),
        doc_lengths,
        dec_x.reshape(8, inner),
        dec_bc.reshape(8, double),
        dec_dt.reshape(8, heads),
    )
    prompt, decoded = pl.pallas_call(
        hand_over,
        out_shape=(
            jax.ShapeDtypeStruct((rows, inner), BF16),
            jax.ShapeDtypeStruct((8, inner), BF16),
        ),
        in_specs=[whole] * 2,
        out_specs=(whole, whole),
        scratch_shapes=[vmem((rows, inner), BF16), vmem((8, inner), BF16), dma((2, 7))],
        compiler_params=pltpu.CompilerParams(vmem_limit_bytes=60 << 20),
    )(prompt, decoded)
    return prompt, decoded.reshape(1, 8, inner)


def solution(mesh):
    placed = (
        P(("group", "seq"), "head"),
        P(("group", "seq"), "head", None),
        P(("group", "seq"), "head"),
        P(None, "head"),
        P(None, "head", None),
        P("head"),
        P("head"),
        P("head"),
        P("head"),
        P("group"),
        P(("group", "seq"), None, "head"),
        P(("group", "seq"), None, "head", None),
        P(("group", "seq"), None, "head"),
    )
    return jax.shard_map(
        body,
        mesh=mesh,
        in_specs=placed,
        out_specs=(P(("group", "seq"), "head"), P(("group", "seq"), None, "head")),
        check_vma=False,
    )
```

```python
import functools

import jax
import jax.numpy as jnp
from jax import lax
from jax.experimental import pallas as pl
from jax.experimental.pallas import tpu as pltpu
from jax.sharding import PartitionSpec as P

BLOCK = 256
TILE = 128
HALO = 16
EPSILON = 1e-05
LOG2E = 1.4426950408889634
MESH = pl.DeviceIdType.MESH
F32 = jnp.float32
BF16 = jnp.bfloat16


def dot(a, b):
    return jnp.dot(a, b, preferred_element_type=F32)


def split3(value):
    high = value.astype(BF16).astype(F32)
    rest = value - high
    middle = rest.astype(BF16).astype(F32)
    low = (rest - middle).astype(BF16).astype(F32)
    return [high, middle, low]


def softplus(value):
    return jnp.maximum(value, 0.0) + jnp.log1p(jnp.exp(-jnp.abs(value)))


def silu(value):
    half = 0.5 * value
    return half + half * jnp.tanh(half)


def conv_chain(rows, taps, linked):
    total = taps[0] * rows
    for tap in taps[1:]:
        total = tap * rows + linked * pltpu.roll(total, 1, 0)
    return total


def kernel(
    seq,
    x_hbm, bc_hbm, dt_hbm, conv_x_hbm, conv_bc_hbm, a_log_hbm, dt_bias_hbm, d_skip_hbm, gain_hbm, doc_hbm,
    dec_x_hbm, dec_bc_hbm, dec_dt_hbm,
    out, dec_out,
    conv_x, conv_bc, a_log, dt_bias, d_skip, gain, doc, dec_x, dec_bc, dec_dt,
    xbuf, bcbuf, dtbuf, rim_msg, rim_recv, tail_recv, tail_f32, xs, xw, bs, cs, bst, expand_a, expand_b, colf, colb, keepb,
    vrow, vecs, enter_q, p_msg, p_recv, s_out, s_in, d_msg, d_recv, c_msg, c_recv, y_msg, y_recv,
    local, keepx, scm, small, dec_factors, obuf, dec_keep, dec_local,
    few_sem, load_sem, rim_ss, rim_rs, tail_ss, tail_rs, p_ss, p_rs, s_ss, s_rs, d_ss, d_rs, c_ss, c_rs, y_ss, y_rs, out_sem,
):
    me = lax.axis_index("seq")
    rows, inner = xs.shape
    blocks = rows // BLOCK
    heads = dtbuf.shape[0]
    width = inner // heads
    pairs = inner // TILE
    state = bs.shape[1]
    docs = doc.shape[0]
    total_rows = rows * seq
    last = seq - 1

    def peer(step):
        return lax.rem(me + step, seq)

    few = [
        (doc_hbm, doc),
        (a_log_hbm, a_log),
        (dt_bias_hbm, dt_bias),
        (d_skip_hbm, d_skip),
        (dt_hbm, dtbuf),
        (conv_x_hbm, conv_x),
        (conv_bc_hbm, conv_bc),
        (gain_hbm, gain),
        (dec_x_hbm, dec_x),
        (dec_bc_hbm, dec_bc),
        (dec_dt_hbm, dec_dt),
    ]
    few = [pltpu.make_async_copy(far, near, few_sem.at[i]) for i, (far, near) in enumerate(few)]
    for copy in few[:5]:
        copy.start()
    loads = []
    for b in reversed(range(blocks)):
        there, here = pl.ds(b * BLOCK, BLOCK), pl.ds(HALO + b * BLOCK, BLOCK)
        loads.append(
            (
                pltpu.make_async_copy(x_hbm.at[there], xbuf.at[here], load_sem.at[2 * b]),
                pltpu.make_async_copy(bc_hbm.at[there], bcbuf.at[here], load_sem.at[2 * b + 1]),
            )
        )

    for copy in loads[0]:
        copy.start()

    barrier = pltpu.get_barrier_semaphore()

    def greet(step, carry):
        pl.semaphore_signal(barrier, inc=1, device_id={"seq": peer(step)}, device_id_type=MESH)
        return carry

    lax.fori_loop(1, seq, greet, 0)

    for copy in few[5:]:
        copy.start()
    for pair in loads[1:]:
        for copy in pair:
            copy.start()

    few[0].wait()
    ends = []
    running = jnp.int32(0)
    for i in range(docs):
        running = running + doc[i]
        ends.append(running)
    base = me * rows

    def start_of(position):
        found = jnp.int32(0)
        for end in ends:
            found = jnp.where(end <= position, jnp.maximum(found, end), found)
        return found

    def next_after(position):
        found = jnp.where(position < 0, jnp.int32(0), jnp.int32(2 * total_rows))
        for end in ends:
            found = jnp.where(end > position, jnp.minimum(found, end), found)
        return found

    def linked_of(positions):
        linked = positions != 0
        for end in ends:
            linked = linked & (positions != end)
        return linked.astype(F32)

    head_row = lax.broadcasted_iota(jnp.int32, (TILE, inner), 0)
    channel = lax.broadcasted_iota(jnp.int32, (TILE, inner), 1)

    def spread(first):
        found = jnp.zeros((TILE, inner), jnp.bool_)
        for copy_at in range(first, first + 3 * heads, heads):
            low = (head_row - copy_at) * width
            found = found | ((channel >= low) & (channel < low + width) & (head_row >= copy_at))
        return found.astype(BF16)

    expand_a[...] = spread(0)
    expand_b[...] = spread(3 * heads)
    upper = (
        lax.broadcasted_iota(jnp.int32, (BLOCK, BLOCK), 0)
        <= lax.broadcasted_iota(jnp.int32, (BLOCK, BLOCK), 1)
    ).astype(BF16)
    lane = lax.broadcasted_iota(jnp.int32, (heads, TILE), 1)

    for copy in few[1:5]:
        copy.wait()
    small[...] = jnp.zeros_like(small)
    small[0:1, 0:heads] = a_log[...]
    small[1:2, 0:heads] = dt_bias[...]
    small[2:3, 0:heads] = d_skip[...]
    columns = small[...].T
    rate = jnp.exp(columns[0:heads, 0:1]) * LOG2E
    bias = columns[0:heads, 1:2]
    skip = columns[0:heads, 2:3]

    steps = [softplus(dtbuf[:, b * BLOCK : (b + 1) * BLOCK] + bias) for b in range(blocks)]
    parts = []
    for step in steps:
        parts += split3(-step * rate)
    sums = dot(jnp.concatenate(parts, axis=0).astype(BF16), upper)
    before = jnp.zeros((heads, 1), F32)
    whole = jnp.ones((heads, 1), F32)
    throughs = []
    dev_next = next_after(base - 1)
    for b in range(blocks):
        at = 3 * b * heads
        cum = sums[at : at + heads] + sums[at + heads : at + 2 * heads] + sums[at + 2 * heads : at + 3 * heads]
        step = steps[b]
        first = base + b * BLOCK
        end = first + BLOCK - 1
        position = first + lax.broadcasted_iota(jnp.int32, (heads, BLOCK), 1)
        cum_end = cum[:, BLOCK - 1 : BLOCK]
        inflow = jnp.where(position >= start_of(end), jnp.exp2(cum_end - cum) * step, 0.0)
        keep_dev = jnp.where(position < dev_next, jnp.exp2(cum + before), 0.0)
        table = jnp.concatenate(
            split3(inflow) + split3(keep_dev) + [cum, jnp.zeros((TILE - 7 * heads, BLOCK), F32)], axis=0
        ).T
        here = pl.ds(b * BLOCK, BLOCK)
        colf[here] = table
        colb[here] = table.astype(BF16)
        vrow[b] = cum - jnp.log2(step)
        block_next = next_after(first - 1)
        keep = jnp.where(position < block_next, jnp.exp2(cum), 0.0)
        keepb[b] = (
            jnp.concatenate(split3(keep) + [jnp.zeros((TILE - 3 * heads, BLOCK), F32)], axis=0)
            .T.astype(BF16)
        )
        throughs.append(jnp.where(end < block_next, jnp.exp2(cum_end), 0.0))
        before = before + cum_end
    whole = jnp.where(base + rows - 1 < dev_next, jnp.exp2(before), 0.0)
    picked = jnp.zeros((heads, TILE), F32)
    for i, column in enumerate([whole, skip] + throughs):
        picked = jnp.where(lane == i, column, picked)
    picked = jnp.concatenate(split3(picked) + [jnp.zeros((TILE - 3 * heads, TILE), F32)], axis=0)
    vecs[...] = dot(picked.T.astype(BF16), expand_a[...])[0:8]

    first_row = lax.broadcasted_iota(jnp.int32, (8, TILE), 0) == 0
    for to in range(seq):
        sides = [vecs[0:1, at : at + TILE] for at in (to // 4 * TILE, to // 4 * TILE + inner // 2)]
        d_msg[to] = jnp.where(first_row, sides[0], sides[1])

    for copy in few[5:]:
        copy.wait()
    for copy in loads[0]:
        copy.wait()
    pl.semaphore_wait(barrier, seq - 1)
    edge = pl.ds(rows, HALO)
    pieces = []
    for buf, count in ((xbuf, inner // TILE), (bcbuf, 2 * state // TILE)):
        for t in range(count):
            pieces.append(buf[edge, t * TILE : (t + 1) * TILE].astype(F32)[HALO - 4 :])
    rim_msg[...] = jnp.concatenate(pieces, axis=0).astype(BF16)

    def rim_copy(to):
        return pltpu.make_async_remote_copy(
            src_ref=rim_msg, dst_ref=rim_recv, send_sem=rim_ss.at[0],
            recv_sem=rim_rs.at[0], device_id={"seq": to}, device_id_type=MESH,
        )

    def tail_copy(to):
        return pltpu.make_async_remote_copy(
            src_ref=rim_msg, dst_ref=tail_recv, send_sem=tail_ss.at[to],
            recv_sem=tail_rs.at[0], device_id={"seq": to}, device_id_type=MESH,
        )

    @pl.when(me < last)
    def _():
        rim_copy(me + 1).start()

    @pl.when(me == last)
    def _():
        def send(step, carry):
            tail_copy(last - step).start()
            return carry

        lax.fori_loop(1, seq, send, 0)
        tail_recv[...] = rim_msg[...]

    @pl.when(me == 0)
    def _():
        rim_recv[...] = jnp.zeros_like(rim_recv)

    def p_copy(part, step, to):
        return pltpu.make_async_remote_copy(
            src_ref=p_msg.at[part, to], dst_ref=p_recv.at[part, me], send_sem=p_ss.at[part, step],
            recv_sem=p_rs.at[part, step], device_id={"seq": to}, device_id_type=MESH,
        )

    def s_copy(part, step, to):
        return pltpu.make_async_remote_copy(
            src_ref=s_out.at[part, to], dst_ref=s_in.at[part, me], send_sem=s_ss.at[part, step],
            recv_sem=s_rs.at[part, step], device_id={"seq": to}, device_id_type=MESH,
        )

    def d_copy(step, to):
        return pltpu.make_async_remote_copy(
            src_ref=d_msg.at[to], dst_ref=d_recv.at[me], send_sem=d_ss.at[step],
            recv_sem=d_rs.at[step], device_id={"seq": to}, device_id_type=MESH,
        )

    def c_copy(step, to):
        return pltpu.make_async_remote_copy(
            src_ref=c_msg.at[lax.rem(lax.div(to, 2), 2)], dst_ref=c_recv.at[me], send_sem=c_ss.at[step],
            recv_sem=c_rs.at[step], device_id={"seq": to}, device_id_type=MESH,
        )

    def y_copy(step, to):
        return pltpu.make_async_remote_copy(
            src_ref=y_msg.at[to], dst_ref=y_recv.at[me], send_sem=y_ss.at[step],
            recv_sem=y_rs.at[step], device_id={"seq": to}, device_id_type=MESH,
        )

    def every(action):
        def body(step, carry):
            action(step, peer(step))
            return carry

        lax.fori_loop(1, seq, body, 0)

    every(lambda step, to: d_copy(step, to).start())
    d_recv[me] = d_msg[me]

    def linked_rows(row):
        positions = base + row - 8 + lax.broadcasted_iota(jnp.int32, (TILE + 8, TILE), 0)
        return linked_of(positions)

    def conv_tile(buf, taps, row, at, linked):
        lanes = slice(at, at + TILE)
        raw = buf[pl.ds(row, TILE + HALO), lanes].astype(F32)[HALO - 8 :]
        return silu(conv_chain(raw, [tap(lanes) for tap in taps], linked)[8:]).astype(BF16)

    x_taps = [lambda lanes, k=k: conv_x[k : k + 1, lanes] for k in range(4)]
    bc_taps = [lambda lanes, k=k: conv_bc[k, :, lanes] for k in range(4)]

    def conv_rows(i, carry):
        row = pl.multiple_of((rows // TILE - 1 - i) * TILE, TILE)

        @pl.when((row == 0) & (me > 0))
        def _():
            rim_copy(me).wait_recv()

        @pl.when(row == 0)
        def _():
            rim = rim_recv[...].astype(F32)
            blank = jnp.zeros((HALO - 4, TILE), F32)
            at = 0
            for buf, count in ((xbuf, inner // TILE), (bcbuf, 2 * state // TILE)):
                for t in range(count):
                    piece = jnp.concatenate([blank, rim[at : at + 4]], axis=0)
                    buf[0:HALO, t * TILE : (t + 1) * TILE] = piece.astype(BF16)
                    at += 4

        here = pl.ds(row, TILE)
        linked = linked_rows(row)
        for at in range(0, state, TILE):
            value = conv_tile(bcbuf, bc_taps, row, at, linked)
            bs[here, at : at + TILE] = value
            bst[at : at + TILE, here] = value.astype(F32).T.astype(BF16)
        scales = colb[here]
        for p in range(pairs):
            lanes = slice(p * TILE, (p + 1) * TILE)
            value = conv_tile(xbuf, x_taps, row, p * TILE, linked)
            xs[here, lanes] = value
            xw[here, lanes] = (value.astype(F32) * dot(scales, expand_a[:, lanes])).astype(BF16)

        return carry

    def conv_c_rows(i, carry):
        row = pl.multiple_of(i * TILE, TILE)
        linked = linked_rows(row)
        for at in range(0, state, TILE):
            cs[pl.ds(row, TILE), at : at + TILE] = conv_tile(bcbuf, bc_taps, row, state + at, linked)
        return carry

    for pair in loads[1:]:
        for copy in pair:
            copy.wait()
    lax.fori_loop(0, rows // TILE, conv_rows, 0, unroll=2)

    enter_q[0] = jnp.zeros((state, inner), BF16)
    share = state // 4

    def contribute(part):
        for g in range(part * pairs // 4, (part + 1) * pairs // 4):
            lanes = slice(g * BLOCK, (g + 1) * BLOCK)
            value = dot(bst[:, 0:BLOCK], xw[0:BLOCK, lanes])
            for b in range(1, blocks):
                here = slice(b * BLOCK, (b + 1) * BLOCK)
                enter_q[b, :, lanes] = value.astype(BF16)
                value = vecs[2 + b : 3 + b, lanes] * value + dot(bst[:, here], xw[here, lanes])
            value = value.astype(BF16)
            for p in range(2):
                for quarter in range(4):
                    to = (8 * g + 4 * p + quarter) % seq
                    p_msg[part, to] = value[quarter * share : (quarter + 1) * share, p * TILE : (p + 1) * TILE]

                    @pl.when(to != me)
                    def _(to=to):
                        p_copy(part, lax.rem(to - me + seq, seq), to).start()

        p_recv[part, me] = p_msg[part, me]

    contribute(0)
    contribute(1)
    lax.fori_loop(0, rows // TILE, conv_c_rows, 0, unroll=2)

    offsets = lax.broadcasted_iota(jnp.int32, (16, TILE), 0)
    tail_doc = jnp.int32(0)
    for end in ends:
        tail_doc = tail_doc + (end <= total_rows - 1).astype(jnp.int32)
    joined = (tail_doc == docs - 1).astype(F32)
    dec_linked = jnp.where(
        offsets < 8, linked_of(total_rows - 8 + offsets), jnp.where(offsets == 8, joined, 1.0)
    )

    def dec_conv(tail_at, given, taps, at):
        lanes = pl.ds(at, TILE)
        ext = jnp.concatenate([tail_f32[pl.ds(tail_at, 8)], given[:, lanes].astype(F32)], axis=0)
        return silu(conv_chain(ext, [tap(lanes) for tap in taps], dec_linked)[8:]).astype(BF16).astype(F32)

    @pl.when(me != last)
    def _():
        tail_copy(me).wait_recv()

    tail = tail_recv[...].astype(F32)
    spaced = []
    for t in range(tail.shape[0] // 4):
        spaced += [jnp.zeros((4, TILE), F32), tail[4 * t : 4 * t + 4]]
    tail_f32[...] = jnp.concatenate(spaced, axis=0)
    dec_bcs = [dec_conv(8 * (pairs + at // TILE), dec_bc, bc_taps, at) for at in range(0, 2 * state, TILE)]

    for i in range(2):
        c_msg[i] = jnp.concatenate([dec_bcs[2 + i], jnp.zeros((8, TILE), F32)], axis=0).astype(BF16)
    every(lambda step, to: c_copy(step, to).start())
    c_recv[me] = c_msg[lax.rem(lax.div(me, 2), 2)]

    def lane_dot(a, b):
        return lax.dot_general(a, b, (((1,), (1,)), ((), ())), preferred_element_type=F32)

    dec_c = jnp.concatenate(dec_bcs[2:], axis=1).astype(BF16)
    dec_b = jnp.concatenate(dec_bcs[:2], axis=1).astype(BF16)
    dec_scores = lane_dot(dec_c, dec_b)
    dec_step = softplus(dec_dt[...] + dt_bias[...])
    dec_cum = -dec_step * jnp.exp(a_log[...])
    dec_row = lax.broadcasted_iota(jnp.int32, (8, heads), 0)
    for shift in (1, 2, 4):
        dec_cum = dec_cum + jnp.where(dec_row >= shift, pltpu.roll(dec_cum, shift, 0), 0.0)
    factors = []
    for s in range(8):
        gap = jnp.where(dec_row >= s, dec_cum - dec_cum[s : s + 1], 0.0)
        weight = dec_scores[:, s : s + 1] * jnp.exp(gap) * dec_step[s : s + 1]
        factors.append(jnp.where(dec_row >= s, weight, 0.0))
    factors.append(jnp.exp(dec_cum))
    factors = jnp.concatenate(factors, axis=0)
    factors = jnp.concatenate(
        split3(factors) + [jnp.zeros((factors.shape[0], TILE - 3 * heads), F32)], axis=1
    ).astype(BF16)
    dec_factors[...] = factors

    def given_pair(p, carry):
        at = pl.multiple_of(p * TILE, TILE)
        lanes = pl.ds(at, TILE)
        wide = dot(dec_factors[...], expand_a[:, lanes])
        given = dec_conv(pl.multiple_of(8 * p, 8), dec_x, x_taps, at)
        answer = vecs[1:2, lanes] * given
        for s in range(8):
            answer = answer + wide[8 * s : 8 * s + 8] * given[s : s + 1]
        dec_local[:, lanes] = answer
        dec_keep[:, lanes] = wide[64:72]
        return carry

    def given_tokens():
        lax.fori_loop(0, pairs, given_pair, 0)


    left_half = lax.broadcasted_iota(jnp.int32, (BLOCK, TILE), 1) < width

    def block_local(b, carry):
        here = pl.ds(pl.multiple_of(b * BLOCK, BLOCK), BLOCK)
        row = lax.broadcasted_iota(jnp.int32, (BLOCK, BLOCK), 0)
        col = lax.broadcasted_iota(jnp.int32, (BLOCK, BLOCK), 1)
        first = base + b * BLOCK
        starts = jnp.zeros((BLOCK, BLOCK), jnp.int32)
        for end in ends:
            starts = jnp.where(row >= end - first, jnp.maximum(starts, end - first), starts)
        scm[...] = jnp.where((col <= row) & (col >= starts), dot(cs[here], bst[:, here]), 0.0)
        top, low = slice(0, TILE), slice(TILE, BLOCK)

        for p in range(pairs):
            lanes = slice(p * TILE, (p + 1) * TILE)
            value = xs[here, lanes]
            zero = jnp.zeros_like(value)
            sides = [jnp.where(left_half, value, zero), jnp.where(left_half, zero, value)]
            tops, lows = [], []
            for side in range(2):
                head = 2 * p + side
                cum_col = colf[here, 6 * heads + head : 6 * heads + head + 1]
                v = vrow[b, head : head + 1, :]
                gap = jnp.minimum(cum_col[top] - v[:, :TILE], 126.0)
                tops.append((scm[top, :TILE] * jnp.exp2(gap)).astype(BF16))
                gap = jnp.minimum(cum_col[low] - v, 126.0)
                lows.append((scm[low, :] * jnp.exp2(gap)).astype(BF16))
            inner_top = dot(
                jnp.concatenate(tops, axis=1), jnp.concatenate([side[top] for side in sides], axis=0)
            )
            inner_low = dot(jnp.concatenate(lows, axis=1), jnp.concatenate(sides, axis=0))
            answer = jnp.concatenate([inner_top, inner_low], axis=0) + vecs[1:2, lanes] * value.astype(F32)
            carried = dot(cs[here], enter_q[b, :, lanes])
            local[here, lanes] = answer + dot(keepb[b], expand_a[:, lanes]) * carried
            keepx[here, lanes] = dot(colb[here], expand_b[:, lanes])
        return carry

    def answer(part):
        def scan(k, value):
            s_out[part, k] = value.astype(BF16)
            return d_recv[k, part : part + 1] * value + p_recv[part, k].astype(F32)

        every(lambda step, to: p_copy(part, step, me).wait_recv())
        final = lax.fori_loop(0, seq, scan, jnp.zeros((share, TILE), F32), unroll=8)
        every(lambda step, to: s_copy(part, step, to).start())
        s_in[part, me] = s_out[part, me]
        return final

    def reply(part, final):
        even = lax.rem(me, 2) == 0
        zero = jnp.zeros_like(final)
        final = jnp.concatenate([jnp.where(even, final, zero), jnp.where(even, zero, final)], axis=0)
        asked = c_recv[...].reshape(seq * HALO, TILE)
        replies = sum(dot(asked, piece.astype(BF16)) for piece in split3(final)).reshape(seq, HALO, TILE)
        y_msg[:, 8 * part : 8 * part + 8] = replies[:, 0:8]

    lax.fori_loop(0, 1, block_local, 0)
    given_tokens()
    lax.fori_loop(1, blocks - 1, block_local, 0)
    every(lambda step, to: d_copy(step, to).wait_recv())
    finals = [answer(0), answer(1)]
    every(lambda step, to: c_copy(step, to).wait_recv())
    for part, final in enumerate(finals):
        reply(part, final)
    every(lambda step, to: y_copy(step, to).start())
    y_recv[me] = y_msg[me]
    lax.fori_loop(blocks - 1, blocks, block_local, 0)

    def carried_part(i, part):
        here = pl.ds(pl.multiple_of(i * TILE, TILE), TILE)
        readout = cs[here]
        pieces = []
        for g in range(pairs // 4):
            entering = jnp.concatenate(
                [
                    jnp.concatenate([s_in[part, 8 * g + 4 * p + t] for t in range(4)], axis=0)
                    for p in range(2)
                ],
                axis=1,
            )
            at = part * inner // 2 + g * BLOCK
            lanes = slice(at, at + BLOCK)
            pieces.append(local[here, lanes] + keepx[here, lanes] * dot(readout, entering))
        squares = sum(piece * piece for piece in pieces)
        return here, pieces, squares[:, :TILE] + squares[:, TILE:]

    def finish_first(i, carry):
        here, pieces, squares = carried_part(i, 0)
        for g, piece in enumerate(pieces):
            local[here, g * BLOCK : (g + 1) * BLOCK] = piece
        colf[here] = squares
        return carry

    def finish(i, carry):
        here, pieces, squares = carried_part(i, 1)
        squares = jnp.sum(squares + colf[here], axis=1, keepdims=True)
        scale = lax.rsqrt(squares / inner + EPSILON)
        for g in range(pairs // 2):
            lanes = slice(g * BLOCK, (g + 1) * BLOCK)
            piece = local[here, lanes] if g < pairs // 4 else pieces[g - pairs // 4]
            obuf[here, lanes] = (piece * scale * gain[:, lanes]).astype(BF16)
        pltpu.make_async_copy(obuf.at[here], out.at[here], out_sem.at[i]).start()
        return carry

    every(lambda step, to: s_copy(0, step, to).wait_recv())
    lax.fori_loop(0, rows // TILE, finish_first, 0, unroll=2)
    every(lambda step, to: s_copy(1, step, to).wait_recv())
    lax.fori_loop(0, rows // TILE, finish, 0, unroll=2)

    every(lambda step, to: y_copy(step, to).wait_recv())
    def norm(pieces):
        squares = sum(piece * piece for piece in pieces)
        scale = lax.rsqrt(jnp.sum(squares, axis=1, keepdims=True) / inner + EPSILON)
        return [piece * scale for piece in pieces]

    pieces = []
    for p in range(pairs):
        lanes = slice(p * TILE, (p + 1) * TILE)
        part, first = 2 * p // pairs, 4 * p % seq
        reading = sum(y_recv[first + t, 8 * part : 8 * part + 8] for t in range(4))
        pieces.append(dec_local[:, lanes] + dec_keep[:, lanes] * reading)
    for p, piece in enumerate(norm(pieces)):
        lanes = slice(p * TILE, (p + 1) * TILE)
        dec_out[:, lanes] = (piece * gain[:, lanes]).astype(BF16)

    @pl.when(me < last)
    def _():
        rim_copy(me + 1).wait_send()

    @pl.when(me == last)
    def _():
        def sent(to, carry):
            tail_copy(to).wait_send()
            return carry

        lax.fori_loop(0, last, sent, 0)

    def settle(step, to):
        for copy in (p_copy, s_copy):
            for part in range(2):
                copy(part, step, to).wait_send()
        for copy in (d_copy, c_copy, y_copy):
            copy(step, to).wait_send()

    every(settle)

    def written(i, carry):
        here = pl.ds(pl.multiple_of(i * TILE, TILE), TILE)
        pltpu.make_async_copy(obuf.at[here], out.at[here], out_sem.at[i]).wait()
        return carry

    lax.fori_loop(0, rows // TILE, written, 0)


def hand_over(held, held_dec, out, out_dec, buf, buf_dec, sem):
    rows = held.shape[0]
    count = sem.shape[1] - 1
    pairs = [((held_dec, buf_dec), (buf_dec, out_dec))]
    for i in range(count):
        here = pl.ds(i * rows // count, rows // count)
        pairs.append(((held.at[here], buf.at[here]), (buf.at[here], out.at[here])))
    copies = [
        [pltpu.make_async_copy(*move, sem.at[way, i]) for way, move in enumerate(moves)]
        for i, moves in enumerate(pairs)
    ]
    for come, _ in copies:
        come.start()
    for come, go in copies:
        come.wait()
        go.start()
    for _, go in copies:
        go.wait()


def body(
    x_in, bc_in, dt_in, conv_x, conv_bc, a_log, dt_bias, d_skip, norm_gain, doc_lengths, dec_x, dec_bc, dec_dt
):
    rows, inner = x_in.shape
    heads = dt_in.shape[1]
    double = bc_in.shape[2]
    state = double // 2
    seq = lax.axis_size("seq")
    blocks = rows // BLOCK
    edge_rows = 4 * (inner + double) // TILE
    whole = pl.BlockSpec(memory_space=pl.ANY)
    near = pl.BlockSpec(memory_space=pltpu.VMEM)
    dma = pltpu.SemaphoreType.DMA
    vmem = pltpu.VMEM
    prompt, decoded = pl.pallas_call(
        functools.partial(kernel, seq),
        out_shape=(
            jax.ShapeDtypeStruct((rows, inner), BF16),
            jax.ShapeDtypeStruct((8, inner), BF16),
        ),
        in_specs=[whole] * 13,
        out_specs=(whole, near),
        scratch_shapes=[
            vmem(conv_x.shape, F32),
            vmem(conv_bc.shape, F32),
            vmem((1, heads), F32),
            vmem((1, heads), F32),
            vmem((1, heads), F32),
            vmem((1, inner), F32),
            pltpu.SMEM(doc_lengths.shape, jnp.int32),
            vmem((8, inner), BF16),
            vmem((8, double), BF16),
            vmem((8, heads), F32),
            vmem((HALO + rows, inner), BF16),
            vmem((HALO + rows, double), BF16),
            vmem((heads, rows), F32),
            vmem((edge_rows, TILE), BF16),
            vmem((edge_rows, TILE), BF16),
            vmem((edge_rows, TILE), BF16),
            vmem((2 * edge_rows, TILE), F32),
            vmem((rows, inner), BF16),
            vmem((rows, inner), BF16),
            vmem((rows, state), BF16),
            vmem((rows, state), BF16),
            vmem((state, rows), BF16),
            vmem((TILE, inner), BF16),
            vmem((TILE, inner), BF16),
            vmem((rows, TILE), F32),
            vmem((rows, TILE), BF16),
            vmem((blocks, BLOCK, TILE), BF16),
            vmem((blocks, heads, BLOCK), F32),
            vmem((8, inner), F32),
            vmem((blocks, state, inner), BF16),
            vmem((2, seq, state // 4, TILE), BF16),
            vmem((2, seq, state // 4, TILE), BF16),
            vmem((2, seq, state // 4, TILE), BF16),
            vmem((2, seq, state // 4, TILE), BF16),
            vmem((seq, 8, TILE), F32),
            vmem((seq, 8, TILE), F32),
            vmem((2, HALO, TILE), BF16),
            vmem((seq, HALO, TILE), BF16),
            vmem((seq, 16, TILE), F32),
            vmem((seq, 16, TILE), F32),
            vmem((rows, inner), F32),
            vmem((rows, inner), F32),
            vmem((BLOCK, BLOCK), F32),
            vmem((TILE, TILE), F32),
            vmem((72, TILE), BF16),
            vmem((rows, inner), BF16),
            vmem((8, inner), F32),
            vmem((8, inner), F32),
            dma((11,)),
            dma((2 * blocks,)),
            dma((1,)),
            dma((1,)),
            dma((seq,)),
            dma((1,)),
        ]
        + [dma((2, seq))] * 4
        + [dma((seq,))] * 6
        + [dma((rows // TILE,))],
        compiler_params=pltpu.CompilerParams(
            collective_id=0, has_side_effects=True, vmem_limit_bytes=60 << 20
        ),
    )(
        x_in,
        bc_in.reshape(rows, double),
        dt_in.T,
        conv_x,
        conv_bc,
        a_log.reshape(1, heads),
        dt_bias.reshape(1, heads),
        d_skip.reshape(1, heads),
        norm_gain.reshape(1, inner),
        doc_lengths,
        dec_x.reshape(8, inner),
        dec_bc.reshape(8, double),
        dec_dt.reshape(8, heads),
    )
    prompt, decoded = pl.pallas_call(
        hand_over,
        out_shape=(
            jax.ShapeDtypeStruct((rows, inner), BF16),
            jax.ShapeDtypeStruct((8, inner), BF16),
        ),
        in_specs=[whole] * 2,
        out_specs=(whole, whole),
        scratch_shapes=[vmem((rows, inner), BF16), vmem((8, inner), BF16), dma((2, 7))],
        compiler_params=pltpu.CompilerParams(vmem_limit_bytes=60 << 20),
    )(prompt, decoded)
    return prompt, decoded.reshape(1, 8, inner)


def solution(mesh):
    placed = (
        P(("group", "seq"), "head"),
        P(("group", "seq"), "head", None),
        P(("group", "seq"), "head"),
        P(None, "head"),
        P(None, "head", None),
        P("head"),
        P("head"),
        P("head"),
        P("head"),
        P("group"),
        P(("group", "seq"), None, "head"),
        P(("group", "seq"), None, "head", None),
        P(("group", "seq"), None, "head"),
    )
    return jax.shard_map(
        body,
        mesh=mesh,
        in_specs=placed,
        out_specs=(P(("group", "seq"), "head"), P(("group", "seq"), None, "head")),
        check_vma=False,
    )
```

```python
import functools

import jax
import jax.numpy as jnp
from jax import lax
from jax.experimental import pallas as pl
from jax.experimental.pallas import tpu as pltpu
from jax.sharding import PartitionSpec as P

BLOCK = 256
TILE = 128
HALO = 16
EPSILON = 1e-05
LOG2E = 1.4426950408889634
MESH = pl.DeviceIdType.MESH
F32 = jnp.float32
BF16 = jnp.bfloat16


def dot(a, b):
    return jnp.dot(a, b, preferred_element_type=F32)


def split3(value):
    high = value.astype(BF16).astype(F32)
    rest = value - high
    middle = rest.astype(BF16).astype(F32)
    low = (rest - middle).astype(BF16).astype(F32)
    return [high, middle, low]


def softplus(value):
    return jnp.maximum(value, 0.0) + jnp.log1p(jnp.exp(-jnp.abs(value)))


def silu(value):
    half = 0.5 * value
    return half + half * jnp.tanh(half)


def conv_chain(rows, taps, linked):
    total = taps[0] * rows
    for tap in taps[1:]:
        total = tap * rows + linked * pltpu.roll(total, 1, 0)
    return total


def kernel(
    seq,
    x_hbm, bc_hbm, dt_hbm, conv_x_hbm, conv_bc_hbm, a_log_hbm, dt_bias_hbm, d_skip_hbm, gain_hbm, doc_hbm,
    dec_x_hbm, dec_bc_hbm, dec_dt_hbm,
    out, dec_out,
    conv_x, conv_bc, a_log, dt_bias, d_skip, gain, doc, dec_x, dec_bc, dec_dt,
    xbuf, bcbuf, dtbuf, rim_msg, rim_recv, tail_recv, tail_f32, xs, xw, bs, cs, bst, expand_a, expand_b, colf, colb, keepb,
    vrow, vecs, enter_q, p_msg, p_recv, s_out, s_in, d_msg, d_recv, c_msg, c_recv, y_msg, y_recv,
    local, keepx, scm, small, dec_factors, shifted, obuf, dec_buf, dec_keep, dec_local,
    few_sem, load_sem, rim_ss, rim_rs, tail_ss, tail_rs, p_ss, p_rs, s_ss, s_rs, d_ss, d_rs, c_ss, c_rs, y_ss, y_rs, out_sem,
):
    me = lax.axis_index("seq")
    rows, inner = xs.shape
    blocks = rows // BLOCK
    heads = dtbuf.shape[0]
    width = inner // heads
    pairs = inner // TILE
    state = bs.shape[1]
    docs = doc.shape[0]
    total_rows = rows * seq
    last = seq - 1

    def peer(step):
        return lax.rem(me + step, seq)

    few = [
        (doc_hbm, doc),
        (a_log_hbm, a_log),
        (dt_bias_hbm, dt_bias),
        (d_skip_hbm, d_skip),
        (dt_hbm, dtbuf),
        (conv_x_hbm, conv_x),
        (conv_bc_hbm, conv_bc),
        (gain_hbm, gain),
        (dec_x_hbm, dec_x),
        (dec_bc_hbm, dec_bc),
        (dec_dt_hbm, dec_dt),
    ]
    few = [pltpu.make_async_copy(far, near, few_sem.at[i]) for i, (far, near) in enumerate(few)]
    for copy in few[:5]:
        copy.start()
    loads = []
    for b in reversed(range(blocks)):
        there, here = pl.ds(b * BLOCK, BLOCK), pl.ds(HALO + b * BLOCK, BLOCK)
        loads.append(
            (
                pltpu.make_async_copy(x_hbm.at[there], xbuf.at[here], load_sem.at[2 * b]),
                pltpu.make_async_copy(bc_hbm.at[there], bcbuf.at[here], load_sem.at[2 * b + 1]),
            )
        )

    for copy in loads[0]:
        copy.start()

    barrier = pltpu.get_barrier_semaphore()

    def greet(step, carry):
        pl.semaphore_signal(barrier, inc=1, device_id={"seq": peer(step)}, device_id_type=MESH)
        return carry

    lax.fori_loop(1, seq, greet, 0)

    for copy in few[5:]:
        copy.start()
    for pair in loads[1:]:
        for copy in pair:
            copy.start()

    few[0].wait()
    ends = []
    running = jnp.int32(0)
    for i in range(docs):
        running = running + doc[i]
        ends.append(running)
    base = me * rows

    def start_of(position):
        found = jnp.int32(0)
        for end in ends:
            found = jnp.where(end <= position, jnp.maximum(found, end), found)
        return found

    def next_after(position):
        found = jnp.where(position < 0, jnp.int32(0), jnp.int32(2 * total_rows))
        for end in ends:
            found = jnp.where(end > position, jnp.minimum(found, end), found)
        return found

    def linked_of(positions):
        linked = positions != 0
        for end in ends:
            linked = linked & (positions != end)
        return linked.astype(F32)

    head_row = lax.broadcasted_iota(jnp.int32, (TILE, inner), 0)
    channel = lax.broadcasted_iota(jnp.int32, (TILE, inner), 1)

    def spread(first):
        found = jnp.zeros((TILE, inner), jnp.bool_)
        for copy_at in range(first, first + 3 * heads, heads):
            low = (head_row - copy_at) * width
            found = found | ((channel >= low) & (channel < low + width) & (head_row >= copy_at))
        return found.astype(BF16)

    expand_a[...] = spread(0)
    expand_b[...] = spread(3 * heads)
    upper = (
        lax.broadcasted_iota(jnp.int32, (BLOCK, BLOCK), 0)
        <= lax.broadcasted_iota(jnp.int32, (BLOCK, BLOCK), 1)
    ).astype(BF16)
    lane = lax.broadcasted_iota(jnp.int32, (heads, TILE), 1)

    for copy in few[1:5]:
        copy.wait()
    small[...] = jnp.zeros_like(small)
    small[0:1, 0:heads] = a_log[...]
    small[1:2, 0:heads] = dt_bias[...]
    small[2:3, 0:heads] = d_skip[...]
    columns = small[...].T
    rate = jnp.exp(columns[0:heads, 0:1]) * LOG2E
    bias = columns[0:heads, 1:2]
    skip = columns[0:heads, 2:3]

    steps = [softplus(dtbuf[:, b * BLOCK : (b + 1) * BLOCK] + bias) for b in range(blocks)]
    parts = []
    for step in steps:
        parts += split3(-step * rate)
    sums = dot(jnp.concatenate(parts, axis=0).astype(BF16), upper)
    before = jnp.zeros((heads, 1), F32)
    whole = jnp.ones((heads, 1), F32)
    throughs = []
    dev_next = next_after(base - 1)
    for b in range(blocks):
        at = 3 * b * heads
        cum = sums[at : at + heads] + sums[at + heads : at + 2 * heads] + sums[at + 2 * heads : at + 3 * heads]
        step = steps[b]
        first = base + b * BLOCK
        end = first + BLOCK - 1
        position = first + lax.broadcasted_iota(jnp.int32, (heads, BLOCK), 1)
        cum_end = cum[:, BLOCK - 1 : BLOCK]
        inflow = jnp.where(position >= start_of(end), jnp.exp2(cum_end - cum) * step, 0.0)
        keep_dev = jnp.where(position < dev_next, jnp.exp2(cum + before), 0.0)
        table = jnp.concatenate(
            split3(inflow) + split3(keep_dev) + [cum, jnp.zeros((TILE - 7 * heads, BLOCK), F32)], axis=0
        ).T
        here = pl.ds(b * BLOCK, BLOCK)
        colf[here] = table
        colb[here] = table.astype(BF16)
        vrow[b] = cum - jnp.log2(step)
        block_next = next_after(first - 1)
        keep = jnp.where(position < block_next, jnp.exp2(cum), 0.0)
        keepb[b] = (
            jnp.concatenate(split3(keep) + [jnp.zeros((TILE - 3 * heads, BLOCK), F32)], axis=0)
            .T.astype(BF16)
        )
        throughs.append(jnp.where(end < block_next, jnp.exp2(cum_end), 0.0))
        before = before + cum_end
    whole = jnp.where(base + rows - 1 < dev_next, jnp.exp2(before), 0.0)
    picked = jnp.zeros((heads, TILE), F32)
    for i, column in enumerate([whole, skip] + throughs):
        picked = jnp.where(lane == i, column, picked)
    picked = jnp.concatenate(split3(picked) + [jnp.zeros((TILE - 3 * heads, TILE), F32)], axis=0)
    vecs[...] = dot(picked.T.astype(BF16), expand_a[...])[0:8]

    first_row = lax.broadcasted_iota(jnp.int32, (8, TILE), 0) == 0
    for to in range(seq):
        sides = [vecs[0:1, at : at + TILE] for at in (to // 4 * TILE, to // 4 * TILE + inner // 2)]
        d_msg[to] = jnp.where(first_row, sides[0], sides[1])

    for copy in few[5:]:
        copy.wait()
    for copy in loads[0]:
        copy.wait()
    pl.semaphore_wait(barrier, seq - 1)
    edge = pl.ds(rows, HALO)
    pieces = []
    for buf, count in ((xbuf, inner // TILE), (bcbuf, 2 * state // TILE)):
        for t in range(count):
            pieces.append(buf[edge, t * TILE : (t + 1) * TILE].astype(F32)[HALO - 4 :])
    rim_msg[...] = jnp.concatenate(pieces, axis=0).astype(BF16)

    def rim_copy(to):
        return pltpu.make_async_remote_copy(
            src_ref=rim_msg, dst_ref=rim_recv, send_sem=rim_ss.at[0],
            recv_sem=rim_rs.at[0], device_id={"seq": to}, device_id_type=MESH,
        )

    def tail_copy(to):
        return pltpu.make_async_remote_copy(
            src_ref=rim_msg, dst_ref=tail_recv, send_sem=tail_ss.at[to],
            recv_sem=tail_rs.at[0], device_id={"seq": to}, device_id_type=MESH,
        )

    @pl.when(me < last)
    def _():
        rim_copy(me + 1).start()

    @pl.when(me == last)
    def _():
        def send(step, carry):
            tail_copy(last - step).start()
            return carry

        lax.fori_loop(1, seq, send, 0)
        tail_recv[...] = rim_msg[...]

    @pl.when(me == 0)
    def _():
        rim_recv[...] = jnp.zeros_like(rim_recv)

    def p_copy(part, step, to):
        return pltpu.make_async_remote_copy(
            src_ref=p_msg.at[part, to], dst_ref=p_recv.at[part, me], send_sem=p_ss.at[part, step],
            recv_sem=p_rs.at[part, step], device_id={"seq": to}, device_id_type=MESH,
        )

    def s_copy(part, step, to):
        return pltpu.make_async_remote_copy(
            src_ref=s_out.at[part, to], dst_ref=s_in.at[part, me], send_sem=s_ss.at[part, step],
            recv_sem=s_rs.at[part, step], device_id={"seq": to}, device_id_type=MESH,
        )

    def d_copy(step, to):
        return pltpu.make_async_remote_copy(
            src_ref=d_msg.at[to], dst_ref=d_recv.at[me], send_sem=d_ss.at[step],
            recv_sem=d_rs.at[step], device_id={"seq": to}, device_id_type=MESH,
        )

    def c_copy(step, to):
        return pltpu.make_async_remote_copy(
            src_ref=c_msg.at[lax.rem(lax.div(to, 2), 2)], dst_ref=c_recv.at[me], send_sem=c_ss.at[step],
            recv_sem=c_rs.at[step], device_id={"seq": to}, device_id_type=MESH,
        )

    def y_copy(step, to):
        return pltpu.make_async_remote_copy(
            src_ref=y_msg.at[to], dst_ref=y_recv.at[me], send_sem=y_ss.at[step],
            recv_sem=y_rs.at[step], device_id={"seq": to}, device_id_type=MESH,
        )

    def every(action):
        def body(step, carry):
            action(step, peer(step))
            return carry

        lax.fori_loop(1, seq, body, 0)

    every(lambda step, to: d_copy(step, to).start())
    d_recv[me] = d_msg[me]

    def linked_rows(row):
        positions = base + row - 8 + lax.broadcasted_iota(jnp.int32, (TILE + 8, TILE), 0)
        one = linked_of(positions)
        two = one * pltpu.roll(one, 1, 0)
        three = one * pltpu.roll(two, 1, 0)
        return [same[8:] for same in (one, two, three)]

    def conv_tile(buf, taps, row, at, linked):
        lanes = slice(at, at + TILE)
        slot = shifted.at[at // TILE + (pairs if buf is bcbuf else 0)]
        raw = buf[pl.ds(row, TILE + HALO), lanes].astype(F32)[HALO - 8 :]
        slot[...] = raw
        total = taps[3](lanes) * raw[8:]
        for back, same in enumerate(linked, 1):
            total = total + taps[3 - back](lanes) * slot[8 - back : 8 - back + TILE] * same
        return silu(total).astype(BF16)

    x_taps = [lambda lanes, k=k: conv_x[k : k + 1, lanes] for k in range(4)]
    bc_taps = [lambda lanes, k=k: conv_bc[k, :, lanes] for k in range(4)]

    def conv_rows(i, carry):
        row = pl.multiple_of((rows // TILE - 1 - i) * TILE, TILE)

        @pl.when((row == 0) & (me > 0))
        def _():
            rim_copy(me).wait_recv()

        @pl.when(row == 0)
        def _():
            rim = rim_recv[...].astype(F32)
            blank = jnp.zeros((HALO - 4, TILE), F32)
            at = 0
            for buf, count in ((xbuf, inner // TILE), (bcbuf, 2 * state // TILE)):
                for t in range(count):
                    piece = jnp.concatenate([blank, rim[at : at + 4]], axis=0)
                    buf[0:HALO, t * TILE : (t + 1) * TILE] = piece.astype(BF16)
                    at += 4

        here = pl.ds(row, TILE)
        linked = linked_rows(row)
        for at in range(0, state, TILE):
            value = conv_tile(bcbuf, bc_taps, row, at, linked)
            bs[here, at : at + TILE] = value
            bst[at : at + TILE, here] = value.astype(F32).T.astype(BF16)
        scales = colb[here]
        for p in range(pairs):
            lanes = slice(p * TILE, (p + 1) * TILE)
            value = conv_tile(xbuf, x_taps, row, p * TILE, linked)
            xs[here, lanes] = value
            xw[here, lanes] = (value.astype(F32) * dot(scales, expand_a[:, lanes])).astype(BF16)

        return carry

    def conv_c_rows(i, carry):
        row = pl.multiple_of(i * TILE, TILE)
        linked = linked_rows(row)
        for at in range(0, state, TILE):
            cs[pl.ds(row, TILE), at : at + TILE] = conv_tile(bcbuf, bc_taps, row, state + at, linked)
        return carry

    for pair in loads[1:]:
        for copy in pair:
            copy.wait()
    lax.fori_loop(0, rows // TILE, conv_rows, 0, unroll=2)

    enter_q[0] = jnp.zeros((state, inner), BF16)
    share = state // 4

    def contribute(part):
        for g in range(part * pairs // 4, (part + 1) * pairs // 4):
            lanes = slice(g * BLOCK, (g + 1) * BLOCK)
            value = dot(bst[:, 0:BLOCK], xw[0:BLOCK, lanes])
            for b in range(1, blocks):
                here = slice(b * BLOCK, (b + 1) * BLOCK)
                enter_q[b, :, lanes] = value.astype(BF16)
                value = vecs[2 + b : 3 + b, lanes] * value + dot(bst[:, here], xw[here, lanes])
            value = value.astype(BF16)
            for p in range(2):
                for quarter in range(4):
                    to = (8 * g + 4 * p + quarter) % seq
                    p_msg[part, to] = value[quarter * share : (quarter + 1) * share, p * TILE : (p + 1) * TILE]

                    @pl.when(to != me)
                    def _(to=to):
                        p_copy(part, lax.rem(to - me + seq, seq), to).start()

        p_recv[part, me] = p_msg[part, me]

    contribute(0)
    contribute(1)
    lax.fori_loop(0, rows // TILE, conv_c_rows, 0, unroll=2)

    offsets = lax.broadcasted_iota(jnp.int32, (16, TILE), 0)
    tail_doc = jnp.int32(0)
    for end in ends:
        tail_doc = tail_doc + (end <= total_rows - 1).astype(jnp.int32)
    joined = (tail_doc == docs - 1).astype(F32)
    dec_linked = jnp.where(
        offsets < 8, linked_of(total_rows - 8 + offsets), jnp.where(offsets == 8, joined, 1.0)
    )

    def dec_conv(tail_at, given, taps, at):
        lanes = pl.ds(at, TILE)
        ext = jnp.concatenate([tail_f32[pl.ds(tail_at, 8)], given[:, lanes].astype(F32)], axis=0)
        return silu(conv_chain(ext, [tap(lanes) for tap in taps], dec_linked)[8:]).astype(BF16).astype(F32)

    @pl.when(me != last)
    def _():
        tail_copy(me).wait_recv()

    tail = tail_recv[...].astype(F32)
    spaced = []
    for t in range(tail.shape[0] // 4):
        spaced += [jnp.zeros((4, TILE), F32), tail[4 * t : 4 * t + 4]]
    tail_f32[...] = jnp.concatenate(spaced, axis=0)
    dec_bcs = [dec_conv(8 * (pairs + at // TILE), dec_bc, bc_taps, at) for at in range(0, 2 * state, TILE)]

    for i in range(2):
        c_msg[i] = jnp.concatenate([dec_bcs[2 + i], jnp.zeros((8, TILE), F32)], axis=0).astype(BF16)
    every(lambda step, to: c_copy(step, to).start())
    c_recv[me] = c_msg[lax.rem(lax.div(me, 2), 2)]

    def lane_dot(a, b):
        return lax.dot_general(a, b, (((1,), (1,)), ((), ())), preferred_element_type=F32)

    dec_c = jnp.concatenate(dec_bcs[2:], axis=1).astype(BF16)
    dec_b = jnp.concatenate(dec_bcs[:2], axis=1).astype(BF16)
    dec_scores = lane_dot(dec_c, dec_b)
    dec_step = softplus(dec_dt[...] + dt_bias[...])
    dec_cum = -dec_step * jnp.exp(a_log[...])
    dec_row = lax.broadcasted_iota(jnp.int32, (8, heads), 0)
    for shift in (1, 2, 4):
        dec_cum = dec_cum + jnp.where(dec_row >= shift, pltpu.roll(dec_cum, shift, 0), 0.0)
    factors = []
    for s in range(8):
        gap = jnp.where(dec_row >= s, dec_cum - dec_cum[s : s + 1], 0.0)
        weight = dec_scores[:, s : s + 1] * jnp.exp(gap) * dec_step[s : s + 1]
        factors.append(jnp.where(dec_row >= s, weight, 0.0))
    factors.append(jnp.exp(dec_cum))
    factors = jnp.concatenate(factors, axis=0)
    factors = jnp.concatenate(
        split3(factors) + [jnp.zeros((factors.shape[0], TILE - 3 * heads), F32)], axis=1
    ).astype(BF16)
    dec_factors[...] = factors

    def given_pair(p, carry):
        at = pl.multiple_of(p * TILE, TILE)
        lanes = pl.ds(at, TILE)
        wide = dot(dec_factors[...], expand_a[:, lanes])
        given = dec_conv(pl.multiple_of(8 * p, 8), dec_x, x_taps, at)
        answer = vecs[1:2, lanes] * given
        for s in range(8):
            answer = answer + wide[8 * s : 8 * s + 8] * given[s : s + 1]
        dec_local[:, lanes] = answer
        dec_keep[:, lanes] = wide[64:72]
        return carry

    def given_tokens():
        lax.fori_loop(0, pairs, given_pair, 0)


    left_half = lax.broadcasted_iota(jnp.int32, (BLOCK, TILE), 1) < width

    def block_local(b, carry):
        here = pl.ds(pl.multiple_of(b * BLOCK, BLOCK), BLOCK)
        row = lax.broadcasted_iota(jnp.int32, (BLOCK, BLOCK), 0)
        col = lax.broadcasted_iota(jnp.int32, (BLOCK, BLOCK), 1)
        first = base + b * BLOCK
        starts = jnp.zeros((BLOCK, BLOCK), jnp.int32)
        for end in ends:
            starts = jnp.where(row >= end - first, jnp.maximum(starts, end - first), starts)
        scm[...] = jnp.where((col <= row) & (col >= starts), dot(cs[here], bst[:, here]), 0.0)
        top, low = slice(0, TILE), slice(TILE, BLOCK)

        for p in range(pairs):
            lanes = slice(p * TILE, (p + 1) * TILE)
            value = xs[here, lanes]
            zero = jnp.zeros_like(value)
            sides = [jnp.where(left_half, value, zero), jnp.where(left_half, zero, value)]
            tops, lows = [], []
            for side in range(2):
                head = 2 * p + side
                cum_col = colf[here, 6 * heads + head : 6 * heads + head + 1]
                v = vrow[b, head : head + 1, :]
                gap = jnp.minimum(cum_col[top] - v[:, :TILE], 126.0)
                tops.append((scm[top, :TILE] * jnp.exp2(gap)).astype(BF16))
                gap = jnp.minimum(cum_col[low] - v, 126.0)
                lows.append((scm[low, :] * jnp.exp2(gap)).astype(BF16))
            inner_top = dot(
                jnp.concatenate(tops, axis=1), jnp.concatenate([side[top] for side in sides], axis=0)
            )
            inner_low = dot(jnp.concatenate(lows, axis=1), jnp.concatenate(sides, axis=0))
            answer = jnp.concatenate([inner_top, inner_low], axis=0) + vecs[1:2, lanes] * value.astype(F32)
            carried = dot(cs[here], enter_q[b, :, lanes])
            local[here, lanes] = answer + dot(keepb[b], expand_a[:, lanes]) * carried
            keepx[here, lanes] = dot(colb[here], expand_b[:, lanes])
        return carry

    def answer(part):
        def scan(k, value):
            s_out[part, k] = value.astype(BF16)
            return d_recv[k, part : part + 1] * value + p_recv[part, k].astype(F32)

        every(lambda step, to: p_copy(part, step, me).wait_recv())
        final = lax.fori_loop(0, seq, scan, jnp.zeros((share, TILE), F32), unroll=8)
        every(lambda step, to: s_copy(part, step, to).start())
        s_in[part, me] = s_out[part, me]
        return final

    def reply(part, final):
        even = lax.rem(me, 2) == 0
        zero = jnp.zeros_like(final)
        final = jnp.concatenate([jnp.where(even, final, zero), jnp.where(even, zero, final)], axis=0)
        asked = c_recv[...].reshape(seq * HALO, TILE)
        replies = sum(dot(asked, piece.astype(BF16)) for piece in split3(final)).reshape(seq, HALO, TILE)
        y_msg[:, 8 * part : 8 * part + 8] = replies[:, 0:8]

    lax.fori_loop(0, 1, block_local, 0)
    given_tokens()
    lax.fori_loop(1, blocks - 1, block_local, 0)
    every(lambda step, to: d_copy(step, to).wait_recv())
    finals = [answer(0), answer(1)]
    every(lambda step, to: c_copy(step, to).wait_recv())
    for part, final in enumerate(finals):
        reply(part, final)
    every(lambda step, to: y_copy(step, to).start())
    y_recv[me] = y_msg[me]
    lax.fori_loop(blocks - 1, blocks, block_local, 0)

    def carried_part(i, part):
        here = pl.ds(pl.multiple_of(i * TILE, TILE), TILE)
        readout = cs[here]
        pieces = []
        for g in range(pairs // 4):
            entering = jnp.concatenate(
                [
                    jnp.concatenate([s_in[part, 8 * g + 4 * p + t] for t in range(4)], axis=0)
                    for p in range(2)
                ],
                axis=1,
            )
            at = part * inner // 2 + g * BLOCK
            lanes = slice(at, at + BLOCK)
            pieces.append(local[here, lanes] + keepx[here, lanes] * dot(readout, entering))
        squares = sum(piece * piece for piece in pieces)
        return here, pieces, squares[:, :TILE] + squares[:, TILE:]

    def finish_first(i, carry):
        here, pieces, squares = carried_part(i, 0)
        for g, piece in enumerate(pieces):
            local[here, g * BLOCK : (g + 1) * BLOCK] = piece
        colf[here] = squares
        return carry

    def finish(i, carry):
        here, pieces, squares = carried_part(i, 1)
        squares = jnp.sum(squares + colf[here], axis=1, keepdims=True)
        scale = lax.rsqrt(squares / inner + EPSILON)
        for g in range(pairs // 2):
            lanes = slice(g * BLOCK, (g + 1) * BLOCK)
            piece = local[here, lanes] if g < pairs // 4 else pieces[g - pairs // 4]
            obuf[here, lanes] = (piece * scale * gain[:, lanes]).astype(BF16)
        pltpu.make_async_copy(obuf.at[here], out.at[here], out_sem.at[i]).start()
        return carry

    @pl.when(me < last)
    def _():
        rim_copy(me + 1).wait_send()

    @pl.when(me == last)
    def _():
        def sent(to, carry):
            tail_copy(to).wait_send()
            return carry

        lax.fori_loop(0, last, sent, 0)

    def settle(step, to):
        for copy in (p_copy, s_copy):
            for part in range(2):
                copy(part, step, to).wait_send()
        for copy in (d_copy, c_copy, y_copy):
            copy(step, to).wait_send()

    every(settle)

    every(lambda step, to: s_copy(0, step, to).wait_recv())
    lax.fori_loop(0, rows // TILE, finish_first, 0, unroll=2)
    every(lambda step, to: s_copy(1, step, to).wait_recv())
    lax.fori_loop(0, rows // TILE - 2, finish, 0, unroll=2)

    every(lambda step, to: y_copy(step, to).wait_recv())
    def norm(pieces):
        squares = sum(piece * piece for piece in pieces)
        scale = lax.rsqrt(jnp.sum(squares, axis=1, keepdims=True) / inner + EPSILON)
        return [piece * scale for piece in pieces]

    pieces = []
    for p in range(pairs):
        lanes = slice(p * TILE, (p + 1) * TILE)
        part, first = 2 * p // pairs, 4 * p % seq
        reading = sum(y_recv[first + t, 8 * part : 8 * part + 8] for t in range(4))
        pieces.append(dec_local[:, lanes] + dec_keep[:, lanes] * reading)
    for p, piece in enumerate(norm(pieces)):
        lanes = slice(p * TILE, (p + 1) * TILE)
        dec_buf[:, lanes] = (piece * gain[:, lanes]).astype(BF16)
    dec_done = pltpu.make_async_copy(dec_buf, dec_out, out_sem.at[rows // TILE])
    dec_done.start()

    lax.fori_loop(rows // TILE - 2, rows // TILE, finish, 0, unroll=2)


    def written(i, carry):
        here = pl.ds(pl.multiple_of(i * TILE, TILE), TILE)
        pltpu.make_async_copy(obuf.at[here], out.at[here], out_sem.at[i]).wait()
        return carry

    lax.fori_loop(0, rows // TILE, written, 0)
    dec_done.wait()


def hand_over(held, held_dec, out, out_dec, buf, buf_dec, sem):
    rows = held.shape[0]
    count = sem.shape[1] - 1
    pairs = [((held_dec, buf_dec), (buf_dec, out_dec))]
    for i in range(count):
        here = pl.ds(i * rows // count, rows // count)
        pairs.append(((held.at[here], buf.at[here]), (buf.at[here], out.at[here])))
    copies = [
        [pltpu.make_async_copy(*move, sem.at[way, i]) for way, move in enumerate(moves)]
        for i, moves in enumerate(pairs)
    ]
    for come, _ in copies:
        come.start()
    for come, go in copies:
        come.wait()
        go.start()
    for _, go in copies:
        go.wait()


def body(
    x_in, bc_in, dt_in, conv_x, conv_bc, a_log, dt_bias, d_skip, norm_gain, doc_lengths, dec_x, dec_bc, dec_dt
):
    rows, inner = x_in.shape
    heads = dt_in.shape[1]
    double = bc_in.shape[2]
    state = double // 2
    seq = lax.axis_size("seq")
    blocks = rows // BLOCK
    edge_rows = 4 * (inner + double) // TILE
    whole = pl.BlockSpec(memory_space=pl.ANY)
    dma = pltpu.SemaphoreType.DMA
    vmem = pltpu.VMEM
    prompt, decoded = pl.pallas_call(
        functools.partial(kernel, seq),
        out_shape=(
            jax.ShapeDtypeStruct((rows, inner), BF16),
            jax.ShapeDtypeStruct((8, inner), BF16),
        ),
        in_specs=[whole] * 13,
        out_specs=(whole, whole),
        scratch_shapes=[
            vmem(conv_x.shape, F32),
            vmem(conv_bc.shape, F32),
            vmem((1, heads), F32),
            vmem((1, heads), F32),
            vmem((1, heads), F32),
            vmem((1, inner), F32),
            pltpu.SMEM(doc_lengths.shape, jnp.int32),
            vmem((8, inner), BF16),
            vmem((8, double), BF16),
            vmem((8, heads), F32),
            vmem((HALO + rows, inner), BF16),
            vmem((HALO + rows, double), BF16),
            vmem((heads, rows), F32),
            vmem((edge_rows, TILE), BF16),
            vmem((edge_rows, TILE), BF16),
            vmem((edge_rows, TILE), BF16),
            vmem((2 * edge_rows, TILE), F32),
            vmem((rows, inner), BF16),
            vmem((rows, inner), BF16),
            vmem((rows, state), BF16),
            vmem((rows, state), BF16),
            vmem((state, rows), BF16),
            vmem((TILE, inner), BF16),
            vmem((TILE, inner), BF16),
            vmem((rows, TILE), F32),
            vmem((rows, TILE), BF16),
            vmem((blocks, BLOCK, TILE), BF16),
            vmem((blocks, heads, BLOCK), F32),
            vmem((8, inner), F32),
            vmem((blocks, state, inner), BF16),
            vmem((2, seq, state // 4, TILE), BF16),
            vmem((2, seq, state // 4, TILE), BF16),
            vmem((2, seq, state // 4, TILE), BF16),
            vmem((2, seq, state // 4, TILE), BF16),
            vmem((seq, 8, TILE), F32),
            vmem((seq, 8, TILE), F32),
            vmem((2, HALO, TILE), BF16),
            vmem((seq, HALO, TILE), BF16),
            vmem((seq, 16, TILE), F32),
            vmem((seq, 16, TILE), F32),
            vmem((rows, inner), F32),
            vmem((rows, inner), F32),
            vmem((BLOCK, BLOCK), F32),
            vmem((TILE, TILE), F32),
            vmem((72, TILE), BF16),
            vmem(((inner + double) // TILE, TILE + 8, TILE), F32),
            vmem((rows, inner), BF16),
            vmem((8, inner), BF16),
            vmem((8, inner), F32),
            vmem((8, inner), F32),
            dma((11,)),
            dma((2 * blocks,)),
            dma((1,)),
            dma((1,)),
            dma((seq,)),
            dma((1,)),
        ]
        + [dma((2, seq))] * 4
        + [dma((seq,))] * 6
        + [dma((rows // TILE + 1,))],
        compiler_params=pltpu.CompilerParams(
            collective_id=0, has_side_effects=True, vmem_limit_bytes=60 << 20
        ),
    )(
        x_in,
        bc_in.reshape(rows, double),
        dt_in.T,
        conv_x,
        conv_bc,
        a_log.reshape(1, heads),
        dt_bias.reshape(1, heads),
        d_skip.reshape(1, heads),
        norm_gain.reshape(1, inner),
        doc_lengths,
        dec_x.reshape(8, inner),
        dec_bc.reshape(8, double),
        dec_dt.reshape(8, heads),
    )
    prompt, decoded = pl.pallas_call(
        hand_over,
        out_shape=(
            jax.ShapeDtypeStruct((rows, inner), BF16),
            jax.ShapeDtypeStruct((8, inner), BF16),
        ),
        in_specs=[whole] * 2,
        out_specs=(whole, whole),
        scratch_shapes=[vmem((rows, inner), BF16), vmem((8, inner), BF16), dma((2, 7))],
        compiler_params=pltpu.CompilerParams(vmem_limit_bytes=60 << 20),
    )(prompt, decoded)
    return prompt, decoded.reshape(1, 8, inner)


def solution(mesh):
    placed = (
        P(("group", "seq"), "head"),
        P(("group", "seq"), "head", None),
        P(("group", "seq"), "head"),
        P(None, "head"),
        P(None, "head", None),
        P("head"),
        P("head"),
        P("head"),
        P("head"),
        P("group"),
        P(("group", "seq"), None, "head"),
        P(("group", "seq"), None, "head", None),
        P(("group", "seq"), None, "head"),
    )
    return jax.shard_map(
        body,
        mesh=mesh,
        in_specs=placed,
        out_specs=(P(("group", "seq"), "head"), P(("group", "seq"), None, "head")),
        check_vma=False,
    )
```
